512 devices in a mesh: expert: 32 (over z, core), fsdp: 16 (over y, x).
Axes of the slice: x: 4, y: 4, z: 16, core: 2. Of those that a mesh axis runs over, the one named last changes fastest.
Arguments:
- tokens: bfloat16 [1024, 4096], P('expert', 'fsdp'), may hold values from -6 to 6
- cotangent: bfloat16 [1024, 4096], P('expert', 'fsdp'), may hold values from -6 to 6
- expert_ids: int32 [1024, 8], P('expert'), may hold values from 0 to 31, as said below
- gate_logits: float32 [1024, 8], P('expert'), may hold values from -6 to 6
- shadow_plan: int32 [32], replicated, may hold values from 0 to 1, as said below
- w_in: bfloat16 [32, 4096, 2, 768], P('expert', 'fsdp'), may hold values from -0.09375 to 0.09375
- w_out: bfloat16 [32, 768, 4096], P('expert', None, 'fsdp'), may hold values from -0.21875 to 0.21875
- mom_in: bfloat16 [32, 4096, 2, 768], P('expert', 'fsdp'), may hold values from -3 to 3
- mom_out: bfloat16 [32, 768, 4096], P('expert', None, 'fsdp'), may hold values from -3 to 3
- in_rows: float32 [32, 2, 4096], P('expert', None, 'fsdp'), may hold values from 1e-05 to 0.01
- in_cols: float32 [32, 2, 2, 768], P('expert'), may hold values from 1e-05 to 0.01
- out_rows: float32 [32, 2, 768], P('expert'), may hold values from 1e-05 to 0.01
- out_cols: float32 [32, 2, 4096], P('expert', None, 'fsdp'), may hold values from 1e-05 to 0.01
Outputs:
- output: bfloat16 [1024, 4096], P('expert', 'fsdp')
- grad_tokens: bfloat16 [1024, 4096], P('expert', 'fsdp')
- new_w_in: bfloat16 [32, 4096, 2, 768], P('expert', 'fsdp')
- new_w_out: bfloat16 [32, 768, 4096], P('expert', None, 'fsdp')
- new_mom_in: bfloat16 [32, 4096, 2, 768], P('expert', 'fsdp')
- new_mom_out: bfloat16 [32, 768, 4096], P('expert', None, 'fsdp')
- new_in_rows: float32 [32, 2, 4096], P('expert', None, 'fsdp')
- new_in_cols: float32 [32, 2, 2, 768], P('expert')
- new_out_rows: float32 [32, 2, 768], P('expert')
- new_out_cols: float32 [32, 2, 4096], P('expert', None, 'fsdp')
The draws below stay inside these ranges and needn't reach their ends.
Inputs may be any that keep to these rules, and one draw needn't show every extreme that they name: `expert_ids`: each row names 8 different experts. `shadow_plan`: exactly 4 entries are 1, one in every run of 8 consecutive experts starting at expert 0, all at the same position within their run; the others 0.
All inputs are finite; a program needn't handle non-finite values.
Results may differ from the reference program's by a relative error of at most 0.0064.
Values may be sent and summed in bfloat16 or wider, within the bound.
A program may use at most 128 MiB of HBM per device.

```python
import math
from functools import partial
import jax
import jax.numpy as jnp
from jax import lax

D = 4096
FF = 768
TOPK = 8
TOK_DEV = 32
EXPERTS = 32
TOKENS = 1024
N_EXPERT = 32


def hot_experts(key):
    start = jax.random.randint(jax.random.fold_in(key, 11), (), 0, 8)
    return (jnp.arange(EXPERTS, dtype=jnp.int32) % 8 == start).astype(jnp.int32)


def draw_expert_ids(key, part):
    marked = hot_experts(key)
    token_noise = jax.random.randint(jax.random.fold_in(key, 23), (TOKENS, EXPERTS), 0, 65536)
    expert_bias = jax.random.randint(jax.random.fold_in(key, 29), (EXPERTS,), 0, 16384)
    scores = (token_noise + expert_bias[None, :] + marked[None, :] * 32768) * EXPERTS + jnp.arange(EXPERTS, dtype=jnp.int32)[None, :]
    chosen = lax.top_k(scores, TOPK)[1]
    return chosen.astype(jnp.int32)


def draw_shadow_plan(key, part):
    return hot_experts(key)


def block_levels(key, dims, cuts, least, top_value):
    gain, own = 1.0, jax.random.fold_in(key, 6)
    for dim, shards_of in cuts:
        steps = jnp.exp(jax.random.uniform(jax.random.fold_in(own, dim), (shards_of,), jnp.float32, least / len(cuts), top_value / len(cuts)))
        gain = gain * jnp.repeat(steps, dims[dim] // shards_of).reshape([-1 if axis == dim else 1 for axis in range(len(dims))])
    return gain


def gaussian(rng, dims, spread, limit, shards=(), kind=jnp.bfloat16):
    entries = spread * jax.random.normal(rng, dims, jnp.float32)
    if shards:
        entries = entries * block_levels(rng, dims, shards, -0.22, 0.18)
    return jnp.clip(entries, -limit, limit).astype(kind)


def setup_inputs(seed: int = 0) -> dict:
    streams_of = jax.random.split(jax.random.key(seed), 14)
    tokens = gaussian(streams_of[0], (TOKENS, D), 1.0, 6.0, ((0, 32), (1, 16)))
    cotangent = gaussian(streams_of[1], (TOKENS, D), 1.0, 6.0, ((0, 32), (1, 16)))
    expert_ids = draw_expert_ids(jax.random.fold_in(streams_of[13], 71), 0)
    gate_logits = gaussian(streams_of[3], (TOKENS, TOPK), 1.5, 6.0, ((0, 32),), jnp.float32)
    shadow_plan = draw_shadow_plan(jax.random.fold_in(streams_of[13], 71), 0)
    w_in = gaussian(streams_of[5], (EXPERTS, D, 2, FF), D ** -0.5, 0.09375, ((0, 32), (1, 16)))
    w_out = gaussian(streams_of[6], (EXPERTS, FF, D), FF ** -0.5, 0.21875, ((0, 32), (2, 16)))
    mom_in = gaussian(streams_of[7], (EXPERTS, D, 2, FF), 0.3, 3.0, ((0, 32), (1, 16)))
    mom_out = gaussian(streams_of[8], (EXPERTS, FF, D), 0.3, 3.0, ((0, 32), (2, 16)))
    in_rows = jnp.clip(jnp.exp(math.log(0.01) - 6.9077553 * jax.random.uniform(streams_of[9], (EXPERTS, 2, D), jnp.float32) ** block_levels(streams_of[9], (EXPERTS, 2, D), ((0, 32), (2, 16)), -0.2, 0.2)), 9.999999747378752e-06, 0.01)
    in_cols = jnp.clip(jnp.exp(math.log(0.01) - 6.9077553 * jax.random.uniform(streams_of[10], (EXPERTS, 2, 2, FF), jnp.float32) ** block_levels(streams_of[10], (EXPERTS, 2, 2, FF), ((0, 32),), -0.2, 0.2)), 9.999999747378752e-06, 0.01)
    out_rows = jnp.clip(jnp.exp(math.log(0.01) - 6.9077553 * jax.random.uniform(streams_of[11], (EXPERTS, 2, FF), jnp.float32) ** block_levels(streams_of[11], (EXPERTS, 2, FF), ((0, 32),), -0.2, 0.2)), 9.999999747378752e-06, 0.01)
    out_cols = jnp.clip(jnp.exp(math.log(0.01) - 6.9077553 * jax.random.uniform(streams_of[12], (EXPERTS, 2, D), jnp.float32) ** block_levels(streams_of[12], (EXPERTS, 2, D), ((0, 32), (2, 16)), -0.2, 0.2)), 9.999999747378752e-06, 0.01)
    return {"tokens": tokens, "cotangent": cotangent, "expert_ids": expert_ids, "gate_logits": gate_logits, "shadow_plan": shadow_plan, "w_in": w_in, "w_out": w_out, "mom_in": mom_in, "mom_out": mom_out, "in_rows": in_rows, "in_cols": in_cols, "out_rows": out_rows, "out_cols": out_cols}


BETA_ONE = 0.9
BETA_TWO = 0.999
BETA_THREE = 0.9999
EPS_ONE = 1e-30
EPS_TWO = 1e-16
CLIP_LIMIT = 1.0
LEARN_RATE = 0.01

def slot_plan(expert_ids, shadow_plan, capacity):
    flat_ids = expert_ids.reshape(-1).astype(jnp.int32)
    expert_count = shadow_plan.shape[0]
    one_hot = (flat_ids[:, None] == jnp.arange(expert_count, dtype=jnp.int32)[None, :]).astype(jnp.int32)
    earlier = (jnp.cumsum(one_hot, axis=0) - one_hot).astype(jnp.int32)
    slot_rank = lax.optimization_barrier(jnp.sum(earlier * one_hot, axis=1)).astype(jnp.int32)
    is_hot = lax.optimization_barrier(jnp.sum(one_hot * shadow_plan[None, :], axis=1)).astype(jnp.int32)
    kept_mask = (slot_rank < capacity) | (is_hot > 0) & (slot_rank < 2 * capacity)
    return (flat_ids, slot_rank, kept_mask)

def came_step(gradient, weight, moment, row_state, col_state):
    squares = gradient * gradient + EPS_ONE
    row_v = BETA_TWO * row_state[0] + (1.0 - BETA_TWO) * lax.optimization_barrier(jnp.mean(squares, axis=1))
    col_v = BETA_TWO * col_state[0] + (1.0 - BETA_TWO) * lax.optimization_barrier(jnp.mean(squares, axis=0))
    scaled = gradient / jnp.sqrt(row_v[:, None] * col_v[None, :] / jnp.mean(row_v))
    scaled = scaled / jnp.maximum(1.0, jnp.sqrt(jnp.mean(scaled * scaled)) / CLIP_LIMIT)
    moment_new = BETA_ONE * moment.astype(jnp.float32) + (1.0 - BETA_ONE) * scaled
    residue = (scaled - moment_new) * (scaled - moment_new) + EPS_TWO
    row_r = BETA_THREE * row_state[1] + (1.0 - BETA_THREE) * lax.optimization_barrier(jnp.mean(residue, axis=1))
    col_r = BETA_THREE * col_state[1] + (1.0 - BETA_THREE) * lax.optimization_barrier(jnp.mean(residue, axis=0))
    stepped = moment_new / jnp.sqrt(row_r[:, None] * col_r[None, :] / jnp.mean(row_r))
    weight_new = (weight.astype(jnp.float32) - LEARN_RATE * stepped).astype(jnp.bfloat16)
    return (weight_new, moment_new.astype(jnp.bfloat16), jnp.stack([row_v, row_r]), jnp.stack([col_v, col_r]))

def reference(tokens, cotangent, expert_ids, gate_logits, shadow_plan, w_in, w_out, mom_in, mom_out, in_rows, in_cols, out_rows, out_cols):
    capacity = TOK_DEV * TOPK // N_EXPERT
    slots = 2 * capacity
    block_slots = N_EXPERT * slots
    grouped = expert_ids.reshape(N_EXPERT, TOK_DEV, TOPK)
    flat_ids, slot_rank, kept_mask = jax.vmap(partial(slot_plan, shadow_plan=shadow_plan, capacity=capacity))(grouped)
    source_index = jnp.arange(N_EXPERT, dtype=jnp.int32)[:, None]
    slot_index = jnp.where(kept_mask, flat_ids * block_slots + source_index * slots + slot_rank, EXPERTS * block_slots).reshape(-1).astype(jnp.int32)
    token_index = (jnp.arange(TOKENS * TOPK, dtype=jnp.int32) // TOPK).astype(jnp.int32)
    slot_token = jnp.full((EXPERTS * block_slots,), TOKENS, jnp.int32).at[slot_index].set(token_index, mode='drop').reshape(EXPERTS, block_slots)
    sig_logits = jax.nn.sigmoid(gate_logits)
    gates = sig_logits / lax.optimization_barrier(jnp.sum(sig_logits, axis=1, keepdims=True))
    pair_gate = jnp.where(kept_mask.reshape(-1), gates.reshape(-1), jnp.zeros_like(gates.reshape(-1)))
    slot_gate = jnp.zeros((EXPERTS * block_slots,), jnp.float32).at[slot_index].set(pair_gate, mode='drop').reshape(EXPERTS, block_slots)
    zero_row = jnp.zeros((1, D), jnp.bfloat16)
    token_table = jnp.concatenate([tokens, zero_row], axis=0)
    cot_table = jnp.concatenate([cotangent, zero_row], axis=0)

    def expert_step(totals, inputs):
        out_total, grad_total = totals
        weight_in, weight_out, moment_in, moment_out, rows_in, cols_in, rows_out, cols_out, token_ids, slot_weights = inputs
        slot_rows = token_table[token_ids]
        flat_in = weight_in.reshape(D, 2 * FF)
        gate_up = jnp.dot(slot_rows, flat_in, preferred_element_type=jnp.float32).reshape(-1, 2, FF)
        gate_pre = gate_up[:, 0]
        up_pre = gate_up[:, 1]
        gate_sig = jax.nn.sigmoid(gate_pre)
        hidden = (gate_pre * gate_sig * up_pre).astype(jnp.bfloat16)
        expert_out = jnp.dot(hidden, weight_out, preferred_element_type=jnp.float32).astype(jnp.bfloat16)
        out_total = out_total.at[token_ids].add(slot_weights[:, None] * expert_out.astype(jnp.float32))
        out_grad = (slot_weights[:, None] * cot_table[token_ids].astype(jnp.float32)).astype(jnp.bfloat16)
        hidden_grad = jnp.dot(out_grad, weight_out.T, preferred_element_type=jnp.float32)
        gate_grad = hidden_grad * up_pre * gate_sig * (1.0 + gate_pre * (1.0 - gate_sig))
        up_grad = hidden_grad * gate_pre * gate_sig
        pre_grad = jnp.stack([gate_grad, up_grad], axis=1).astype(jnp.bfloat16).reshape(-1, 2 * FF)
        in_grad = jnp.dot(pre_grad, flat_in.T, preferred_element_type=jnp.float32).astype(jnp.bfloat16)
        grad_total = grad_total.at[token_ids].add(in_grad.astype(jnp.float32))
        grad_in = jnp.dot(slot_rows.T, pre_grad, preferred_element_type=jnp.float32)
        grad_out = jnp.dot(hidden.T, out_grad, preferred_element_type=jnp.float32)
        new_in = came_step(grad_in, flat_in, moment_in.reshape(D, 2 * FF), rows_in, cols_in.reshape(2, 2 * FF))
        new_out = came_step(grad_out, weight_out, moment_out, rows_out, cols_out)
        return ((out_total, grad_total), (new_in[0].reshape(D, 2, FF), new_in[1].reshape(D, 2, FF), new_in[2], new_in[3].reshape(2, 2, FF), new_out[0], new_out[1], new_out[2], new_out[3]))
    start_totals = (jnp.zeros((TOKENS + 1, D), jnp.float32), jnp.zeros((TOKENS + 1, D), jnp.float32))
    final_totals, new_state = lax.scan(expert_step, start_totals, (w_in, w_out, mom_in, mom_out, in_rows, in_cols, out_rows, out_cols, slot_token, slot_gate))
    output = final_totals[0][:TOKENS].astype(jnp.bfloat16)
    grad_tokens = final_totals[1][:TOKENS].astype(jnp.bfloat16)
    return (output, grad_tokens, new_state[0], new_state[4], new_state[1], new_state[5], new_state[2], new_state[3], new_state[6], new_state[7])
```

```python
import functools

import jax
import jax.numpy as jnp
from jax import lax
from jax.experimental import pallas as pl
from jax.experimental.pallas import tpu as pltpu
from jax.sharding import PartitionSpec as P

BETA_ONE = 0.9
BETA_TWO = 0.999
BETA_THREE = 0.9999
EPS_ONE = 1e-30
EPS_TWO = 1e-16
CLIP_LIMIT = 1.0
LEARN_RATE = 0.01

MESH = pl.DeviceIdType.MESH
F32 = jnp.float32
BF16 = jnp.bfloat16
NE = 32
CAP = 8
SIDE = 4
T = 32
DL = 256
FF = 768
ROWS = NE * CAP
TILE = ROWS // (SIDE * SIDE)
COLS = 3 * FF
NSTAT = 1280
HALF = COLS // 2


def nn(a, b):
    return jnp.dot(a, b, preferred_element_type=F32)


def nt(a, b):
    return lax.dot_general(a, b, (((1,), (1,)), ((), ())), preferred_element_type=F32)


def tn(a, b):
    return lax.dot_general(a, b, (((0,), (0,)), ((), ())), preferred_element_type=F32)


def iota(shape, dim):
    return lax.broadcasted_iota(jnp.int32, shape, dim)


def one_hot(cond):
    return jnp.where(cond, 1.0, 0.0).astype(BF16)


def to_column(v):
    n = v.shape[1]
    return jnp.sum(jnp.where(iota((n, n), 0) == iota((n, n), 1), v, 0.0), axis=1, keepdims=True)


def to_row(v):
    n = v.shape[0]
    return jnp.sum(jnp.where(iota((n, n), 0) == iota((n, n), 1), v, 0.0), axis=0, keepdims=True)


def pack(rows):
    n = rows.shape[0] // CAP
    left = rows[:, :128].reshape(n, CAP, 128)
    right = rows[:, 128:].reshape(n, CAP, 128)
    return jnp.concatenate([left, right], axis=1).astype(BF16)


def unpack(blocks):
    wide = blocks.astype(F32)
    n = wide.shape[0]
    left = wide[:, :CAP].reshape(n * CAP, 128)
    right = wide[:, CAP:].reshape(n * CAP, 128)
    return jnp.concatenate([left, right], axis=1).astype(BF16)


def all_of(view, sem):
    pltpu.make_async_copy(view, view, sem).wait()


def main_kernel(
    mark,
    tokens, cotangent, ids, logits, plan, w_in, w_out, mom_in, mom_out, in_rows, out_cols,
    output, grad_tokens, grads, w_cat, m_cat, sums, row_v,
    send_x, send_c, recv_x, recv_c, x_rows, c_rows, x_t, c_t, parts, got_a, got_b, mid_a, mid_b, acc_a, acc_b,
    last_a, last_b, units, send_o, send_i, recv_o, recv_i, recv_o1, recv_i1, pick, pick1, gated, gated1,
    stat, stat_x, stat_y, pre_tile, ssem, rsem,
):
    me = lax.axis_index("expert")
    fs = lax.axis_index("fsdp")
    my, mx = fs // SIDE, lax.rem(fs, SIDE)
    stride, off = (1, 0) if mark is None else (NE // 4, mark)
    n_hot = NE // stride
    hot = None if mark is None else lax.rem(me, stride) == off

    def when_hot(f):
        if hot is None:
            f()
        else:
            pl.when(hot)(f)

    def both(f):
        f(0)
        when_hot(lambda: f(1))

    def x_peer(d):
        return (me, my * SIDE + lax.rem(mx + d, SIDE))

    def y_peer(d):
        return (me, lax.rem(my + d, SIDE) * SIDE + mx)

    def remote(src, dst, k, dev):
        pltpu.make_async_remote_copy(
            src_ref=src, dst_ref=dst, send_sem=ssem.at[k], recv_sem=rsem.at[k],
            device_id=dev, device_id_type=MESH,
        ).start()

    barrier = pltpu.get_barrier_semaphore()

    @pl.loop(1, NE)
    def _(i):
        pl.semaphore_signal(
            barrier, inc=1, device_id=(lax.rem(me + i, NE), fs), device_id_type=MESH
        )

    for d in range(1, SIDE):
        pl.semaphore_signal(barrier, inc=1, device_id=x_peer(d), device_id_type=MESH)
        pl.semaphore_signal(barrier, inc=1, device_id=y_peer(d), device_id_type=MESH)

    expert = iota((NE, T), 0)
    chosen = jnp.zeros((NE, T), F32)
    gate_of = jnp.zeros((NE, T), F32)
    sig = jax.nn.sigmoid(logits[...])
    gates = sig / jnp.sum(sig, axis=0, keepdims=True)
    picks = ids[...]
    for k in range(ids.shape[0]):
        hit = picks[k : k + 1, :] == expert
        chosen = jnp.where(hit, 1.0, chosen)
        gate_of = jnp.where(hit, gates[k : k + 1, :], gate_of)
    earlier = one_hot(iota((T, T), 0) < iota((T, T), 1))
    rank = jnp.where(chosen > 0.0, nn(chosen.astype(BF16), earlier), 1e6)
    marked = jnp.sum(
        jnp.where(iota((NE, NE), 0) == iota((NE, NE), 1), plan[...], 0), axis=1, keepdims=True
    )
    rank_hot = jnp.where(marked > 0, rank - CAP, 1e6)

    def selection(rank_block, gate_block, pick_ref, gated_ref, sx, sc):
        n = rank_block.shape[0]
        slot = iota((n, CAP, T), 1).astype(F32)
        sel = jnp.where(rank_block[:, None, :] == slot, 1.0, 0.0)
        wsel = (sel * gate_block[:, None, :]).reshape(n * CAP, T)
        sel = sel.reshape(n * CAP, T)
        pick_ref[...] = sel
        gated_ref[...] = wsel
        sel16 = sel.astype(BF16)
        sx[0:n] = pack(nn(sel16, tokens[...]))
        sc[0:n] = pack(nn(sel16, cotangent[...]) * jnp.sum(wsel, axis=1, keepdims=True))

    selection(rank, gate_of, pick, gated, send_x.at[0], send_c.at[0])
    if mark is None:
        rank1, gate1 = rank_hot, gate_of
    else:
        rank1 = jnp.concatenate([rank_hot[e : e + 1] for e in range(off, NE, stride)], axis=0)
        gate1 = jnp.concatenate([gate_of[e : e + 1] for e in range(off, NE, stride)], axis=0)
    selection(rank1, gate1, pick1, gated1, send_x.at[1], send_c.at[1])

    pl.semaphore_wait(barrier, NE - 1 + 2 * (SIDE - 1))

    def dispatch(src, dst, k):
        pltpu.make_async_copy(src.at[0, me], dst.at[0, me], rsem.at[k]).start()

        @pl.loop(1, NE)
        def _(i):
            to = lax.rem(me + i, NE)
            remote(src.at[0, to], dst.at[0, me], k, (to, fs))

        @pl.loop(0, n_hot)
        def _(i):
            r = lax.rem(i + me, n_hot)
            to = r * stride + off

            @pl.when(to == me)
            def _():
                pltpu.make_async_copy(src.at[1, r], dst.at[1, me], rsem.at[k + 1]).start()

            @pl.when(to != me)
            def _():
                remote(src.at[1, r], dst.at[1, me], k + 1, (to, fs))

    dispatch(send_x, recv_x, 0)
    dispatch(send_c, recv_c, 2)

    even = one_hot(iota((DL, 2 * DL), 1) == 2 * iota((DL, 2 * DL), 0))
    odd = one_hot(iota((DL, 2 * DL), 1) == 2 * iota((DL, 2 * DL), 0) + 1)
    eye = one_hot(iota((DL, DL), 0) == iota((DL, DL), 1))

    def split(w2, w3, into):
        flat = w2.reshape(2 * DL, FF)

        @pl.loop(0, FF // 256)
        def _(c):
            c0 = pl.multiple_of(c * 256, 256)
            piece = flat[:, pl.ds(c0, 256)]
            into[:, pl.ds(c0, 256)] = nn(even, piece).astype(BF16)
            into[:, pl.ds(c0 + FF, 256)] = nn(odd, piece).astype(BF16)
            into[:, pl.ds(c0 + 2 * FF, 256)] = nt(eye, w3[0, pl.ds(c0, 256), :]).astype(BF16)

    split(w_in, w_out, w_cat)

    def part_cols(q):
        return (0, FF) if q == 0 else (2 * FF, FF // 2)

    def got_cols(q):
        return (0, FF) if q == 0 else (FF, FF // 2)

    def project(b, q):
        src, rows_ref, t_ref = (recv_x, x_rows, x_t) if q == 0 else (recv_c, c_rows, c_t)
        all_of(src.at[b], rsem.at[2 * q + b])
        rows = unpack(src[b])
        rows_ref[b] = rows
        start, width = part_cols(q)

        @pl.loop(0, 2 * width // 256)
        def _(c):
            c0 = pl.multiple_of(start + c * 256, 256)
            piece = nn(rows_ref[b], w_cat[:, pl.ds(c0, 256)])
            parts[b, :, :, :, pl.ds(c0, 256)] = piece.reshape(SIDE, SIDE, TILE, 256).astype(BF16)

        g0, _w = got_cols(q)
        for d in range(1, SIDE):
            to_x, to_y = lax.rem(mx + d, SIDE), lax.rem(my + d, SIDE)
            remote(
                parts.at[b, :, to_x, :, pl.ds(start, width)],
                got_a.at[b, d - 1, :, :, pl.ds(g0, width)], 8 + 4 * q + 2 * b, x_peer(d),
            )
            remote(
                parts.at[b, to_y, :, :, pl.ds(start + width, width)],
                got_b.at[b, d - 1, :, :, pl.ds(g0, width)], 9 + 4 * q + 2 * b, y_peer(d),
            )

    def halfway(b, q):
        start, width = part_cols(q)
        g0, _w = got_cols(q)
        cols = pl.ds(g0, width)
        for half in range(2):
            got, mid, acc, last = (
                (got_a, mid_a, acc_a, last_a) if half == 0 else (got_b, mid_b, acc_b, last_b)
            )
            k = 8 + 4 * q + 2 * b + half
            all_of(got.at[b, :, :, :, cols], rsem.at[k])
            if half == 0:
                own = parts[b, :, mx, :, pl.ds(start, width)]
            else:
                own = parts[b, my, :, :, pl.ds(start + width, width)]
            total = own.astype(F32)
            for d in range(SIDE - 1):
                total = total + got[b, d, :, :, cols].astype(F32)
            acc[b, :, :, cols] = total
            mid[b, :, :, cols] = total.astype(BF16)
            for d in range(1, SIDE):
                to = lax.rem((my if half == 0 else mx) + d, SIDE)
                remote(
                    mid.at[b, to, :, cols], last.at[b, d - 1, :, cols], k + 8,
                    y_peer(d) if half == 0 else x_peer(d),
                )

    def finished(b, q, half):
        g0, width = got_cols(q)
        cols = pl.ds(g0, width)
        acc, last = (acc_a, last_a) if half == 0 else (acc_b, last_b)
        all_of(last.at[b, :, :, cols], rsem.at[16 + 4 * q + 2 * b + half])
        total = acc[b, my if half == 0 else mx, :, cols]
        for d in range(SIDE - 1):
            total = total + last[b, d, :, cols].astype(F32)
        return total

    def unit_cols(q):
        return (2 * FF, FF // 2) if q == 0 else (0, FF)

    def share(b, q):
        c0, width = unit_cols(q)
        first, second = pl.ds(c0, width), pl.ds(c0 + width, width)
        for d in range(1, SIDE):
            a, z = units.at[b, my, mx, :, first], units.at[b, my, mx, :, second]
            remote(a, a, 24 + 4 * q + 2 * b, y_peer(d))
            remote(z, z, 25 + 4 * q + 2 * b, x_peer(d))

    def spread(b, q):
        c0, width = unit_cols(q)
        first, second = pl.ds(c0, width), pl.ds(c0 + width, width)
        k = 24 + 4 * q + 2 * b
        all_of(units.at[b, 0:3, 0, :, first], rsem.at[k])
        a = units.at[b, :, mx, :, first]
        for d in range(1, SIDE):
            remote(a, a, k + 8, x_peer(d))
        all_of(units.at[b, 0, 0:3, :, second], rsem.at[k + 1])
        z = units.at[b, my, :, :, second]
        for d in range(1, SIDE):
            remote(z, z, k + 9, y_peer(d))

    def gathered(b, q):
        c0, width = unit_cols(q)
        for half in range(2):
            all_of(
                units.at[b, :, 0:3, :, pl.ds(c0 + half * width, width)],
                rsem.at[32 + 4 * q + 2 * b + half],
            )

    def forward(b):
        gate_pre, up_pre = finished(b, 0, 0), finished(b, 0, 1)
        s = jax.nn.sigmoid(gate_pre)
        pre_tile[b, 0] = gate_pre
        pre_tile[b, 1] = up_pre
        units[b, my, mx, :, 2 * FF : 3 * FF] = (gate_pre * s * up_pre).astype(BF16)
        share(b, 0)

    def backward(b):
        hidden_grad = jnp.concatenate([finished(b, 1, 0), finished(b, 1, 1)], axis=1)
        gate_pre, up_pre = pre_tile[b, 0], pre_tile[b, 1]
        s = jax.nn.sigmoid(gate_pre)
        gate_grad = hidden_grad * up_pre * s * (1.0 + gate_pre * (1.0 - s))
        units[b, my, mx, :, 0:FF] = gate_grad.astype(BF16)
        units[b, my, mx, :, FF : 2 * FF] = (hidden_grad * gate_pre * s).astype(BF16)
        share(b, 1)

    def give_back(b, src, dst0, dst1, k):
        if b == 0:
            pltpu.make_async_copy(src.at[0, me], dst0.at[me], rsem.at[k]).start()
        else:
            pltpu.make_async_copy(src.at[1, me], dst1.at[me // stride], rsem.at[k + 1]).start()

        @pl.loop(1, NE)
        def _(i):
            to = lax.rem(me + i, NE)
            if b == 0:
                remote(src.at[0, to], dst0.at[me], k, (to, fs))
            else:
                remote(src.at[1, to], dst1.at[me // stride], k + 1, (to, fs))

    def rows_of(b, start, width):
        return units[b, :, :, :, start : start + width].reshape(ROWS, width)

    def down(b):
        gathered(b, 0)
        out = nt(rows_of(b, 2 * FF, FF), w_cat[:, 2 * FF : 3 * FF])
        send_o[b] = pack(out)
        give_back(b, send_o, recv_o, recv_o1, 40)

    def up(b):
        gathered(b, 1)
        out = nt(rows_of(b, 0, 2 * FF), w_cat[:, 0 : 2 * FF])
        send_i[b] = pack(out)
        give_back(b, send_i, recv_i, recv_i1, 42)

    both(lambda b: project(b, 0))
    both(lambda b: project(b, 1))
    split(mom_in, mom_out, m_cat)
    both(lambda b: halfway(b, 0))
    both(lambda b: halfway(b, 1))
    both(forward)
    both(backward)

    def transposes(b):
        x_t[b] = x_rows[b].astype(F32).T.astype(BF16)
        c_t[b] = c_rows[b].astype(F32).T.astype(BF16)

    both(transposes)
    both(lambda b: spread(b, 0))
    both(lambda b: spread(b, 1))
    both(down)
    both(up)

    def gradients(b):
        @pl.loop(0, COLS // 256)
        def _(c):
            cols = pl.ds(pl.multiple_of(c * 256, 256), 256)
            right = units[b, :, :, :, cols].reshape(ROWS, 256)

            def put(left):
                g = nn(left, right)
                if b == 0:
                    grads[:, cols] = g
                else:
                    grads[:, cols] = grads[:, cols] + g

            @pl.when(c < 2 * FF // 256)
            def _():
                put(x_t[b])

            @pl.when(c >= 2 * FF // 256)
            def _():
                put(c_t[b])

    both(gradients)

    def square_rows(c0, n):
        def step(c, total):
            g = grads[:, pl.ds(pl.multiple_of(c0 + c * 128, 128), 128)]
            return total + g * g

        total = lax.fori_loop(0, n // 128, step, jnp.zeros((DL, 128), F32))
        return jnp.sum(total, axis=1, keepdims=True) / n + EPS_ONE

    kept_in = to_column(in_rows[0, 0:1, :])
    kept_out = to_column(out_cols[0, 0:1, :])
    v_in = BETA_TWO * kept_in + (1.0 - BETA_TWO) * square_rows(0, 2 * FF)
    v_out = BETA_TWO * kept_out + (1.0 - BETA_TWO) * square_rows(2 * FF, FF)
    row_v[...] = jnp.where(iota((DL, 128), 1) == 0, v_in, v_out)
    root_in, root_out = lax.rsqrt(v_in), lax.rsqrt(v_out)

    def column_sums(c, carry):
        cols = pl.ds(pl.multiple_of(c * 128, 128), 128)
        g = grads[:, cols]
        m = m_cat[:, cols].astype(F32)
        r = jnp.where(c < 2 * FF // 128, root_in, root_out)
        gr = g * r
        four = [jnp.sum(v, axis=0, keepdims=True) for v in (g * g, gr * gr, gr * m, m * m)]
        low = c >= HALF // 128
        at = pl.ds(pl.multiple_of((c - jnp.where(low, HALF // 128, 0)) * 128, 128), 128)
        block = jnp.concatenate(four, axis=0)

        @pl.when(low)
        def _():
            stat[4:8, at] = block

        @pl.when(jnp.logical_not(low))
        def _():
            stat[0:4, at] = block

        return carry

    lax.fori_loop(0, COLS // 128, column_sums, 0)
    total_v = jnp.sum(v_in, axis=0, keepdims=True)
    total_r = jnp.sum(in_rows[0, 1:2, :], axis=1, keepdims=True)
    stat[:, HALF:NSTAT] = jnp.where(iota((8, NSTAT - HALF), 0) == 0, total_v, total_r)

    mid = NSTAT // 2
    one, two = pl.ds(0, mid), pl.ds(mid, mid)
    stat_x[mx, :, one] = stat[:, one]
    stat_y[my, :, two] = stat[:, two]
    for d in range(1, SIDE):
        remote(stat.at[:, one], stat_x.at[mx, :, one], 44, x_peer(d))
        remote(stat.at[:, two], stat_y.at[my, :, two], 45, y_peer(d))
    all_of(stat_x.at[0:3, :, one], rsem.at[44])
    part = stat_x[0, :, one] + stat_x[1, :, one] + stat_x[2, :, one] + stat_x[3, :, one]
    stat_y[my, :, one] = part
    for d in range(1, SIDE):
        mine = stat_y.at[my, :, one]
        remote(mine, mine, 46, y_peer(d))
    all_of(stat_y.at[0:3, :, two], rsem.at[45])
    part = stat_y[0, :, two] + stat_y[1, :, two] + stat_y[2, :, two] + stat_y[3, :, two]
    stat_x[mx, :, two] = part
    for d in range(1, SIDE):
        mine = stat_x.at[mx, :, two]
        remote(mine, mine, 47, x_peer(d))

    def combine(weights, recv, exact):
        rows = unpack(recv[...])
        if exact:
            return tn(weights.astype(BF16), rows)
        high = weights.astype(BF16)
        low = (weights - high.astype(F32)).astype(BF16)
        return tn(high, rows) + tn(low, rows)

    all_of(recv_o, rsem.at[40])
    all_of(recv_o1, rsem.at[41])
    output[...] = (
        combine(gated[...], recv_o, False) + combine(gated1[...], recv_o1, False)
    ).astype(BF16)
    all_of(recv_i, rsem.at[42])
    all_of(recv_i1, rsem.at[43])
    grad_tokens[...] = (
        combine(pick[...], recv_i, True) + combine(pick1[...], recv_i1, True)
    ).astype(BF16)

    all_of(stat_y.at[0:3, :, one], rsem.at[46])
    sums[:, one] = stat_y[0, :, one] + stat_y[1, :, one] + stat_y[2, :, one] + stat_y[3, :, one]
    all_of(stat_x.at[0:3, :, two], rsem.at[47])
    sums[:, two] = stat_x[0, :, two] + stat_x[1, :, two] + stat_x[2, :, two] + stat_x[3, :, two]

    for q, src in ((0, send_x), (1, send_c)):
        all_of(src.at[0, 0 : NE - 1], ssem.at[2 * q])
        if mark is None:
            all_of(src.at[1, 0 : NE - 1], ssem.at[2 * q + 1])
        else:
            pl.when(hot)(lambda: all_of(src.at[1, 0 : n_hot - 1], ssem.at[2 * q + 1]))
            pl.when(jnp.logical_not(hot))(lambda: all_of(src.at[1, 0:n_hot], ssem.at[2 * q + 1]))

    def sent(b):
        for q in range(2):
            _s, width = part_cols(q)
            g0, _w = got_cols(q)
            c0, uw = unit_cols(q)
            cols = pl.ds(g0, width)
            for half in range(2):
                k = 4 * q + 2 * b + half
                got, last = (got_a, last_a) if half == 0 else (got_b, last_b)
                all_of(got.at[b, :, :, :, cols], ssem.at[8 + k])
                all_of(last.at[b, :, :, cols], ssem.at[16 + k])
                ucols = pl.ds(c0 + half * uw, uw)
                all_of(units.at[b, 0, 0:3, :, ucols], ssem.at[24 + k])
                all_of(units.at[b, :, 0:3, :, ucols], ssem.at[32 + k])
        all_of(send_o.at[b, 0 : NE - 1], ssem.at[40 + b])
        all_of(send_i.at[b, 0 : NE - 1], ssem.at[42 + b])

    both(sent)
    for k in range(4):
        all_of(stat_x.at[0:3, :, one], ssem.at[44 + k])


def update_kernel(
    grads, w_cat, m_cat, sums, row_v, out16, grad16, in_rows, in_cols, out_rows, out_cols,
    output, grad_tokens, new_w_in, new_w_out, new_mom_in, new_mom_out,
    new_in_rows, new_in_cols, new_out_rows, new_out_cols, moment, w16, m16,
):
    output[...] = out16[...]
    grad_tokens[...] = grad16[...]
    full = DL * SIDE * SIDE
    n_in, n_out = 2 * FF, FF

    def line(k):
        return jnp.concatenate([sums[k : k + 1, 0:HALF], sums[4 + k : 5 + k, 0:HALF]], axis=1)

    sq, sq_scaled, cross, sq_mom = line(0), line(1), line(2), line(3)
    sum_v = sums[0:1, HALF : HALF + 1]
    sum_r = sums[1:2, HALF : HALF + 1]

    def state(k):
        return jnp.concatenate(
            [in_cols[0, k, 0:1, :], in_cols[0, k, 1:2, :], out_rows[0, k : k + 1, :]], axis=1
        )

    v_in, v_out = row_v[:, 0:1], row_v[:, 1:2]
    col_v = BETA_TWO * state(0) + (1.0 - BETA_TWO) * (sq / full + EPS_ONE)
    is_in = iota((1, COLS), 1) < n_in

    def total(v):
        low = jnp.sum(v[:, 0:n_in], axis=1, keepdims=True)
        return low, jnp.sum(v[:, n_in:COLS], axis=1, keepdims=True)

    mean_in = sum_v / full
    mean_out = total(col_v)[1] / n_out
    inv = 1.0 / col_v
    norm_in, norm_out = total(sq_scaled * inv)
    clip_in = jnp.maximum(1.0, jnp.sqrt(norm_in * mean_in / (full * n_in)) / CLIP_LIMIT)
    clip_out = jnp.maximum(1.0, jnp.sqrt(norm_out * mean_out / (full * n_out)) / CLIP_LIMIT)
    scale = jnp.where(is_in, jnp.sqrt(mean_in) / clip_in, jnp.sqrt(mean_out) / clip_out)
    col_s = scale * lax.rsqrt(col_v)
    keep = BETA_ONE * BETA_ONE
    residue = keep * (col_s * col_s * sq_scaled - 2.0 * col_s * cross + sq_mom) + full * EPS_TWO
    col_r = BETA_THREE * state(1) + (1.0 - BETA_THREE) * residue / full
    mean_r_in = BETA_THREE * sum_r / full + (1.0 - BETA_THREE) * total(residue)[0] / (full * n_in)
    mean_r_out = total(col_r)[1] / n_out
    root_in, root_out = lax.rsqrt(v_in), lax.rsqrt(v_out)

    def first(c0, root, scale_row):
        acc = jnp.zeros((DL, 128), F32)
        for c in range(scale_row.shape[1] // 128):
            cols = slice(c0 + c * 128, c0 + (c + 1) * 128)
            u = grads[:, cols] * root * scale_row[:, c * 128 : (c + 1) * 128]
            old = m_cat[:, cols].astype(F32)
            new = BETA_ONE * old + (1.0 - BETA_ONE) * u
            diff = u - new
            acc = acc + (diff * diff + EPS_TWO)
            moment[:, cols] = new
            m16[:, cols] = new.astype(BF16)
        return jnp.sum(acc, axis=1, keepdims=True)

    res_in = first(0, root_in, col_s[:, 0:n_in])
    res_out = first(n_in, root_out, col_s[:, n_in:COLS])
    r_in = (
        BETA_THREE * to_column(in_rows[0, 1:2, :]) + (1.0 - BETA_THREE) * res_in / n_in
    )
    r_out = (
        BETA_THREE * to_column(out_cols[0, 1:2, :]) + (1.0 - BETA_THREE) * res_out / n_out
    )
    step_in, step_out = LEARN_RATE * lax.rsqrt(r_in), LEARN_RATE * lax.rsqrt(r_out)
    col_step = lax.rsqrt(col_r) * jnp.where(is_in, jnp.sqrt(mean_r_in), jnp.sqrt(mean_r_out))
    for c in range(COLS // 128):
        cols = slice(c * 128, (c + 1) * 128)
        rows = step_in if c < n_in // 128 else step_out
        w16[:, cols] = (
            w_cat[:, cols].astype(F32) - moment[:, cols] * rows * col_step[:, cols]
        ).astype(BF16)

    even = one_hot(iota((2 * DL, DL), 0) == 2 * iota((2 * DL, DL), 1))
    odd = one_hot(iota((2 * DL, DL), 0) == 2 * iota((2 * DL, DL), 1) + 1)
    eye = one_hot(iota((DL, DL), 0) == iota((DL, DL), 1))
    for src, inner, outer in ((w16, new_w_in, new_w_out), (m16, new_mom_in, new_mom_out)):
        flat = inner.reshape(2 * DL, FF)
        for c in range(FF // 256):
            lo = slice(c * 256, (c + 1) * 256)
            hi = slice(FF + c * 256, FF + (c + 1) * 256)
            flat[:, lo] = (nn(even, src[:, lo]) + nn(odd, src[:, hi])).astype(BF16)
            third = slice(2 * FF + c * 256, 2 * FF + (c + 1) * 256)
            outer[0, lo, :] = nt(eye, src[:, third]).astype(BF16)

    new_in_rows[0, 0:1, :] = to_row(v_in)
    new_in_rows[0, 1:2, :] = to_row(r_in)
    new_out_cols[0, 0:1, :] = to_row(v_out)
    new_out_cols[0, 1:2, :] = to_row(r_out)
    for k, v in ((0, col_v), (1, col_r)):
        new_in_cols[0, k, 0:1, :] = v[:, 0:FF]
        new_in_cols[0, k, 1:2, :] = v[:, FF : 2 * FF]
        new_out_rows[0, k : k + 1, :] = v[:, 2 * FF :]


def vmem():
    return pl.BlockSpec(memory_space=pltpu.VMEM)


def main_call(mark, *operands):
    n_hot = NE if mark is None else 4
    sds = jax.ShapeDtypeStruct
    outs = (
        sds((T, DL), BF16),
        sds((T, DL), BF16),
        sds((DL, COLS), F32),
        sds((DL, COLS), BF16),
        sds((DL, COLS), BF16),
        sds((8, NSTAT), F32),
        sds((DL, 128), F32),
    )
    block = (2, NE, 2 * CAP, 128)
    wide = COLS // 2
    scratch = [
        pltpu.VMEM(block, BF16),
        pltpu.VMEM(block, BF16),
        pltpu.VMEM(block, BF16),
        pltpu.VMEM(block, BF16),
        pltpu.VMEM((2, ROWS, DL), BF16),
        pltpu.VMEM((2, ROWS, DL), BF16),
        pltpu.VMEM((2, DL, ROWS), BF16),
        pltpu.VMEM((2, DL, ROWS), BF16),
        pltpu.VMEM((2, SIDE, SIDE, TILE, COLS), BF16),
        pltpu.VMEM((2, SIDE - 1, SIDE, TILE, wide), BF16),
        pltpu.VMEM((2, SIDE - 1, SIDE, TILE, wide), BF16),
        pltpu.VMEM((2, SIDE, TILE, wide), BF16),
        pltpu.VMEM((2, SIDE, TILE, wide), BF16),
        pltpu.VMEM((2, SIDE, TILE, wide), F32),
        pltpu.VMEM((2, SIDE, TILE, wide), F32),
        pltpu.VMEM((2, SIDE - 1, TILE, wide), BF16),
        pltpu.VMEM((2, SIDE - 1, TILE, wide), BF16),
        pltpu.VMEM((2, SIDE, SIDE, TILE, COLS), BF16),
        pltpu.VMEM(block, BF16),
        pltpu.VMEM(block, BF16),
        pltpu.VMEM((NE, 2 * CAP, 128), BF16),
        pltpu.VMEM((NE, 2 * CAP, 128), BF16),
        pltpu.VMEM((n_hot, 2 * CAP, 128), BF16),
        pltpu.VMEM((n_hot, 2 * CAP, 128), BF16),
        pltpu.VMEM((ROWS, T), F32),
        pltpu.VMEM((n_hot * CAP, T), F32),
        pltpu.VMEM((ROWS, T), F32),
        pltpu.VMEM((n_hot * CAP, T), F32),
        pltpu.VMEM((8, NSTAT), F32),
        pltpu.VMEM((SIDE, 8, NSTAT), F32),
        pltpu.VMEM((SIDE, 8, NSTAT), F32),
        pltpu.VMEM((2, 2, TILE, FF), F32),
        pltpu.SemaphoreType.DMA((48,)),
        pltpu.SemaphoreType.DMA((48,)),
    ]
    return pl.pallas_call(
        functools.partial(main_kernel, mark),
        out_shape=outs,
        in_specs=[vmem()] * len(operands),
        out_specs=tuple(vmem() for _ in outs),
        scratch_shapes=scratch,
        compiler_params=pltpu.CompilerParams(
            collective_id=0 if mark is None else 1 + mark,
            has_side_effects=True,
            vmem_limit_bytes=48 * 2**20,
        ),
    )(*operands)


def per_device(
    tokens, cotangent, expert_ids, gate_logits, shadow_plan, w_in, w_out, mom_in, mom_out,
    in_rows, in_cols, out_rows, out_cols,
):
    operands = (
        tokens, cotangent, expert_ids.T, gate_logits.T, shadow_plan.reshape(1, -1),
        w_in, w_out, mom_in, mom_out, in_rows, out_cols,
    )
    out16, grad16, grads, w_cat, m_cat, sums, row_v = main_call(None, *operands)
    sds = jax.ShapeDtypeStruct
    outs = (
        sds(tokens.shape, BF16),
        sds(tokens.shape, BF16),
        sds(w_in.shape, BF16),
        sds(w_out.shape, BF16),
        sds(w_in.shape, BF16),
        sds(w_out.shape, BF16),
        sds(in_rows.shape, F32),
        sds(in_cols.shape, F32),
        sds(out_rows.shape, F32),
        sds(out_cols.shape, F32),
    )
    return pl.pallas_call(
        update_kernel,
        out_shape=outs,
        in_specs=[vmem()] * 11,
        out_specs=tuple(vmem() for _ in outs),
        scratch_shapes=[
            pltpu.VMEM((DL, COLS), F32),
            pltpu.VMEM((DL, COLS), BF16),
            pltpu.VMEM((DL, COLS), BF16),
        ],
        compiler_params=pltpu.CompilerParams(vmem_limit_bytes=48 * 2**20),
    )(grads, w_cat, m_cat, sums, row_v, out16, grad16, in_rows, in_cols, out_rows, out_cols)


def solution(mesh):
    both = P("expert", "fsdp")
    rows3 = P("expert", "fsdp", None, None)
    cols3 = P("expert", None, "fsdp")
    own = P("expert", None)
    return jax.shard_map(
        per_device,
        mesh=mesh,
        in_specs=(
            both, both, own, own, P(), rows3, cols3, rows3, cols3,
            cols3, P("expert", None, None, None), P("expert", None, None), cols3,
        ),
        out_specs=(
            both, both, rows3, cols3, rows3, cols3,
            cols3, P("expert", None, None, None), P("expert", None, None), cols3,
        ),
        check_vma=False,
    )
```

```python
import functools

import jax
import jax.numpy as jnp
from jax import lax
from jax.experimental import pallas as pl
from jax.experimental.pallas import tpu as pltpu
from jax.sharding import PartitionSpec as P

BETA_ONE = 0.9
BETA_TWO = 0.999
BETA_THREE = 0.9999
EPS_ONE = 1e-30
EPS_TWO = 1e-16
CLIP_LIMIT = 1.0
LEARN_RATE = 0.01

MESH = pl.DeviceIdType.MESH
F32 = jnp.float32
BF16 = jnp.bfloat16
NE = 32
CAP = 8
RUN = 8
SIDE = 4
T = 32
DL = 256
FF = 768
ROWS = NE * CAP
TILE = ROWS // (SIDE * SIDE)
COLS = 3 * FF
NSTAT = 1280
HALF = COLS // 2


def nn(a, b):
    return jnp.dot(a, b, preferred_element_type=F32)


def nt(a, b):
    return lax.dot_general(a, b, (((1,), (1,)), ((), ())), preferred_element_type=F32)


def tn(a, b):
    return lax.dot_general(a, b, (((0,), (0,)), ((), ())), preferred_element_type=F32)


def iota(shape, dim):
    return lax.broadcasted_iota(jnp.int32, shape, dim)


def one_hot(cond):
    return jnp.where(cond, 1.0, 0.0).astype(BF16)


def to_column(v):
    n = v.shape[1]
    return jnp.sum(jnp.where(iota((n, n), 0) == iota((n, n), 1), v, 0.0), axis=1, keepdims=True)


def to_row(v):
    n = v.shape[0]
    return jnp.sum(jnp.where(iota((n, n), 0) == iota((n, n), 1), v, 0.0), axis=0, keepdims=True)


def pack(rows):
    n = rows.shape[0] // CAP
    left = rows[:, :128].reshape(n, CAP, 128)
    right = rows[:, 128:].reshape(n, CAP, 128)
    return jnp.concatenate([left, right], axis=1).astype(BF16)


def unpack(blocks):
    wide = blocks.astype(F32)
    n = wide.shape[0]
    left = wide[:, :CAP].reshape(n * CAP, 128)
    right = wide[:, CAP:].reshape(n * CAP, 128)
    return jnp.concatenate([left, right], axis=1).astype(BF16)


def all_of(view, sem):
    pltpu.make_async_copy(view, view, sem).wait()


def main_kernel(
    mark,
    tokens_h, cotangent_h, ids_h, logits_h, w_in_h, w_out_h, mom_in_h, mom_out_h, in_rows_h, out_cols_h,
    output, grad_tokens, grads, w_cat, m_cat, sums, row_v,
    tokens, cotangent, ids, logits, w_in, w_out, mom_in, mom_out, in_rows, out_cols, load_sem,
    send_x, send_c, recv_x, recv_c, x_rows, c_rows, x_t, c_t, parts, got_a, got_b, mid_a, mid_b, acc_a, acc_b,
    last_a, last_b, units, send_o, send_i, recv_o, recv_i, recv_o1, recv_i1, pick, pick1, gated, gated1,
    stat, stat_x, stat_y, pre_tile, ssem, rsem,
):
    me = lax.axis_index("expert")
    fs = lax.axis_index("fsdp")
    my, mx = fs // SIDE, lax.rem(fs, SIDE)
    stride, off = RUN, mark
    n_hot = NE // stride
    hot = lax.rem(me, stride) == off
    when_hot = pl.when(hot)

    def both(f):
        f(0)
        when_hot(lambda: f(1))

    def x_peer(d):
        return (me, my * SIDE + lax.rem(mx + d, SIDE))

    def y_peer(d):
        return (me, lax.rem(my + d, SIDE) * SIDE + mx)

    def remote(src, dst, k, dev):
        pltpu.make_async_remote_copy(
            src_ref=src, dst_ref=dst, send_sem=ssem.at[k], recv_sem=rsem.at[k],
            device_id=dev, device_id_type=MESH,
        ).start()

    loads = [
        pltpu.make_async_copy(src, dst, load_sem.at[i])
        for i, (src, dst) in enumerate((
            (ids_h, ids), (logits_h, logits), (tokens_h, tokens), (cotangent_h, cotangent),
            (w_in_h.reshape(2 * DL, FF), w_in), (w_out_h, w_out),
            (mom_in_h.reshape(2 * DL, FF), mom_in), (mom_out_h, mom_out),
            (in_rows_h, in_rows), (out_cols_h, out_cols),
        ))
    ]
    for load in loads:
        load.start()

    barrier = pltpu.get_barrier_semaphore()

    @pl.loop(1, NE)
    def _(i):
        pl.semaphore_signal(
            barrier, inc=1, device_id=(lax.rem(me + i, NE), fs), device_id_type=MESH
        )

    for d in range(1, SIDE):
        pl.semaphore_signal(barrier, inc=1, device_id=x_peer(d), device_id_type=MESH)
        pl.semaphore_signal(barrier, inc=1, device_id=y_peer(d), device_id_type=MESH)

    for load in loads[:4]:
        load.wait()
    expert = iota((NE, T), 0)
    chosen = jnp.zeros((NE, T), F32)
    gate_of = jnp.zeros((NE, T), F32)
    sig = jax.nn.sigmoid(logits[...])
    gates = sig / jnp.sum(sig, axis=0, keepdims=True)
    picks = ids[...]
    for k in range(ids.shape[0]):
        hit = picks[k : k + 1, :] == expert
        chosen = jnp.where(hit, 1.0, chosen)
        gate_of = jnp.where(hit, gates[k : k + 1, :], gate_of)
    earlier = one_hot(iota((T, T), 0) < iota((T, T), 1))
    rank = jnp.where(chosen > 0.0, nn(chosen.astype(BF16), earlier), 1e6)
    rank_hot = rank - CAP

    def selection(rank_block, gate_block, pick_ref, gated_ref, sx, sc):
        n = rank_block.shape[0]
        slot = iota((n, CAP, T), 1).astype(F32)
        sel = jnp.where(rank_block[:, None, :] == slot, 1.0, 0.0)
        wsel = (sel * gate_block[:, None, :]).reshape(n * CAP, T)
        sel = sel.reshape(n * CAP, T)
        pick_ref[...] = sel
        gated_ref[...] = wsel
        sel16 = sel.astype(BF16)
        sx[0:n] = pack(nn(sel16, tokens[...]))
        sc[0:n] = pack(nn(sel16, cotangent[...]) * jnp.sum(wsel, axis=1, keepdims=True))

    selection(rank, gate_of, pick, gated, send_x.at[0], send_c.at[0])
    rank1 = jnp.concatenate([rank_hot[e : e + 1] for e in range(off, NE, stride)], axis=0)
    gate1 = jnp.concatenate([gate_of[e : e + 1] for e in range(off, NE, stride)], axis=0)
    selection(rank1, gate1, pick1, gated1, send_x.at[1], send_c.at[1])

    pl.semaphore_wait(barrier, NE - 1 + 2 * (SIDE - 1))

    def dispatch(src, dst, k):
        pltpu.make_async_copy(src.at[0, me], dst.at[0, me], rsem.at[k]).start()

        @pl.loop(1, NE)
        def _(i):
            to = lax.rem(me + i, NE)
            remote(src.at[0, to], dst.at[0, me], k, (to, fs))

        @pl.loop(0, n_hot)
        def _(i):
            r = lax.rem(i + me, n_hot)
            to = r * stride + off

            @pl.when(to == me)
            def _():
                pltpu.make_async_copy(src.at[1, r], dst.at[1, me], rsem.at[k + 1]).start()

            @pl.when(to != me)
            def _():
                remote(src.at[1, r], dst.at[1, me], k + 1, (to, fs))

    dispatch(send_x, recv_x, 0)
    dispatch(send_c, recv_c, 2)

    even = one_hot(iota((DL, 2 * DL), 1) == 2 * iota((DL, 2 * DL), 0))
    odd = one_hot(iota((DL, 2 * DL), 1) == 2 * iota((DL, 2 * DL), 0) + 1)
    eye = one_hot(iota((DL, DL), 0) == iota((DL, DL), 1))

    def split(w2, w3, into):
        @pl.loop(0, FF // 256)
        def _(c):
            c0 = pl.multiple_of(c * 256, 256)
            piece = w2[:, pl.ds(c0, 256)]
            into[:, pl.ds(c0, 256)] = nn(even, piece).astype(BF16)
            into[:, pl.ds(c0 + FF, 256)] = nn(odd, piece).astype(BF16)
            into[:, pl.ds(c0 + 2 * FF, 256)] = nt(eye, w3[0, pl.ds(c0, 256), :]).astype(BF16)

    loads[4].wait()
    loads[5].wait()
    split(w_in, w_out, w_cat)

    def part_cols(q):
        return (0, FF) if q == 0 else (2 * FF, FF // 2)

    def got_cols(q):
        return (0, FF) if q == 0 else (FF, FF // 2)

    def project(b, q):
        src, rows_ref, t_ref = (recv_x, x_rows, x_t) if q == 0 else (recv_c, c_rows, c_t)
        all_of(src.at[b], rsem.at[2 * q + b])
        rows = unpack(src[b])
        rows_ref[b] = rows.reshape(SIDE, SIDE, TILE, DL)
        start, width = part_cols(q)

        @pl.loop(0, 2 * width // 256)
        def _(c):
            c0 = pl.multiple_of(start + c * 256, 256)
            piece = nn(rows, w_cat[:, pl.ds(c0, 256)])
            parts[b, :, :, :, pl.ds(c0, 256)] = piece.reshape(SIDE, SIDE, TILE, 256).astype(BF16)

        g0, _w = got_cols(q)
        for d in range(1, SIDE):
            to_x, to_y = lax.rem(mx + d, SIDE), lax.rem(my + d, SIDE)
            remote(
                parts.at[b, :, to_x, :, pl.ds(start, width)],
                got_a.at[b, d - 1, :, :, pl.ds(g0, width)], 8 + 4 * q + 2 * b, x_peer(d),
            )
            remote(
                parts.at[b, to_y, :, :, pl.ds(start + width, width)],
                got_b.at[b, d - 1, :, :, pl.ds(g0, width)], 9 + 4 * q + 2 * b, y_peer(d),
            )

    def halfway(b, q):
        start, width = part_cols(q)
        g0, _w = got_cols(q)
        cols = pl.ds(g0, width)
        for half in range(2):
            got, mid, acc, last = (
                (got_a, mid_a, acc_a, last_a) if half == 0 else (got_b, mid_b, acc_b, last_b)
            )
            k = 8 + 4 * q + 2 * b + half
            rows_ref = x_rows if q == 0 else c_rows
            tiles = rows_ref.at[b, :, mx] if half == 0 else rows_ref.at[b, my]
            own = nn(
                tiles[...].reshape(SIDE * TILE, DL),
                w_cat[:, start + half * width : start + (half + 1) * width],
            )
            all_of(got.at[b, :, :, :, cols], rsem.at[k])
            total = own.reshape(SIDE, TILE, width)
            for d in range(SIDE - 1):
                total = total + got[b, d, :, :, cols].astype(F32)
            acc[b, :, :, cols] = total
            mid[b, :, :, cols] = total.astype(BF16)
            for d in range(1, SIDE):
                to = lax.rem((my if half == 0 else mx) + d, SIDE)
                remote(
                    mid.at[b, to, :, cols], last.at[b, d - 1, :, cols], k + 8,
                    y_peer(d) if half == 0 else x_peer(d),
                )

    def finished(b, q, half):
        g0, width = got_cols(q)
        cols = pl.ds(g0, width)
        acc, last = (acc_a, last_a) if half == 0 else (acc_b, last_b)
        all_of(last.at[b, :, :, cols], rsem.at[16 + 4 * q + 2 * b + half])
        total = acc[b, my if half == 0 else mx, :, cols]
        for d in range(SIDE - 1):
            total = total + last[b, d, :, cols].astype(F32)
        return total

    def unit_cols(q):
        return (2 * FF, FF // 2) if q == 0 else (0, FF)

    def share(b, q):
        c0, width = unit_cols(q)
        first, second = pl.ds(c0, width), pl.ds(c0 + width, width)
        for d in range(1, SIDE):
            a, z = units.at[b, my, mx, :, first], units.at[b, my, mx, :, second]
            remote(a, a, 24 + 4 * q + 2 * b, y_peer(d))
            remote(z, z, 25 + 4 * q + 2 * b, x_peer(d))

    def spread(b, q):
        c0, width = unit_cols(q)
        first, second = pl.ds(c0, width), pl.ds(c0 + width, width)
        k = 24 + 4 * q + 2 * b
        all_of(units.at[b, 0:3, 0, :, first], rsem.at[k])
        a = units.at[b, :, mx, :, first]
        for d in range(1, SIDE):
            remote(a, a, k + 8, x_peer(d))
        all_of(units.at[b, 0, 0:3, :, second], rsem.at[k + 1])
        z = units.at[b, my, :, :, second]
        for d in range(1, SIDE):
            remote(z, z, k + 9, y_peer(d))

    def gathered(b, q):
        c0, width = unit_cols(q)
        for half in range(2):
            all_of(
                units.at[b, :, 0:3, :, pl.ds(c0 + half * width, width)],
                rsem.at[32 + 4 * q + 2 * b + half],
            )

    def forward(b):
        gate_pre, up_pre = finished(b, 0, 0), finished(b, 0, 1)
        s = jax.nn.sigmoid(gate_pre)
        pre_tile[b, 0] = gate_pre
        pre_tile[b, 1] = up_pre
        units[b, my, mx, :, 2 * FF : 3 * FF] = (gate_pre * s * up_pre).astype(BF16)
        share(b, 0)

    def backward(b):
        hidden_grad = jnp.concatenate([finished(b, 1, 0), finished(b, 1, 1)], axis=1)
        gate_pre, up_pre = pre_tile[b, 0], pre_tile[b, 1]
        s = jax.nn.sigmoid(gate_pre)
        gate_grad = hidden_grad * up_pre * s * (1.0 + gate_pre * (1.0 - s))
        units[b, my, mx, :, 0:FF] = gate_grad.astype(BF16)
        units[b, my, mx, :, FF : 2 * FF] = (hidden_grad * gate_pre * s).astype(BF16)
        share(b, 1)

    def give_back(b, src, dst0, dst1, k):
        if b == 0:
            pltpu.make_async_copy(src.at[0, me], dst0.at[me], rsem.at[k]).start()
        else:
            pltpu.make_async_copy(src.at[1, me], dst1.at[me // stride], rsem.at[k + 1]).start()

        @pl.loop(1, NE)
        def _(i):
            to = lax.rem(me + i, NE)
            if b == 0:
                remote(src.at[0, to], dst0.at[me], k, (to, fs))
            else:
                remote(src.at[1, to], dst1.at[me // stride], k + 1, (to, fs))

    def rows_of(b, start, width):
        return units[b, :, :, :, start : start + width].reshape(ROWS, width)

    def down(b):
        gathered(b, 0)
        out = nt(rows_of(b, 2 * FF, FF), w_cat[:, 2 * FF : 3 * FF])
        send_o[b] = pack(out)
        give_back(b, send_o, recv_o, recv_o1, 40)

    def up(b):
        gathered(b, 1)
        out = nt(rows_of(b, 0, 2 * FF), w_cat[:, 0 : 2 * FF])
        send_i[b] = pack(out)
        give_back(b, send_i, recv_i, recv_i1, 42)

    both(lambda b: project(b, 0))
    both(lambda b: project(b, 1))
    for load in loads[6:]:
        load.wait()
    split(mom_in, mom_out, m_cat)
    both(lambda b: halfway(b, 0))
    both(lambda b: halfway(b, 1))
    both(forward)
    both(backward)

    def transposes(b):
        x_t[b] = x_rows[b].reshape(ROWS, DL).astype(F32).T.astype(BF16)
        c_t[b] = c_rows[b].reshape(ROWS, DL).astype(F32).T.astype(BF16)

    both(transposes)
    both(lambda b: spread(b, 0))
    both(lambda b: spread(b, 1))
    both(down)
    both(up)

    def gradients(b):
        @pl.loop(0, COLS // 256)
        def _(c):
            cols = pl.ds(pl.multiple_of(c * 256, 256), 256)
            right = units[b, :, :, :, cols].reshape(ROWS, 256)

            def put(left):
                g = nn(left, right)
                if b == 0:
                    grads[:, cols] = g
                else:
                    grads[:, cols] = grads[:, cols] + g

            @pl.when(c < 2 * FF // 256)
            def _():
                put(x_t[b])

            @pl.when(c >= 2 * FF // 256)
            def _():
                put(c_t[b])

    both(gradients)

    def square_rows(c0, n):
        def step(c, total):
            g = grads[:, pl.ds(pl.multiple_of(c0 + c * 128, 128), 128)]
            return total + g * g

        total = lax.fori_loop(0, n // 128, step, jnp.zeros((DL, 128), F32))
        return jnp.sum(total, axis=1, keepdims=True) / n + EPS_ONE

    kept_in = to_column(in_rows[0, 0:1, :])
    kept_out = to_column(out_cols[0, 0:1, :])
    v_in = BETA_TWO * kept_in + (1.0 - BETA_TWO) * square_rows(0, 2 * FF)
    v_out = BETA_TWO * kept_out + (1.0 - BETA_TWO) * square_rows(2 * FF, FF)
    row_v[...] = jnp.where(iota((DL, 128), 1) == 0, v_in, v_out)
    root_in, root_out = lax.rsqrt(v_in), lax.rsqrt(v_out)

    def column_sums(c, carry):
        cols = pl.ds(pl.multiple_of(c * 128, 128), 128)
        g = grads[:, cols]
        m = m_cat[:, cols].astype(F32)
        r = jnp.where(c < 2 * FF // 128, root_in, root_out)
        gr = g * r
        four = [jnp.sum(v, axis=0, keepdims=True) for v in (g * g, gr * gr, gr * m, m * m)]
        low = c >= HALF // 128
        at = pl.ds(pl.multiple_of((c - jnp.where(low, HALF // 128, 0)) * 128, 128), 128)
        block = jnp.concatenate(four, axis=0)

        @pl.when(low)
        def _():
            stat[4:8, at] = block

        @pl.when(jnp.logical_not(low))
        def _():
            stat[0:4, at] = block

        return carry

    lax.fori_loop(0, COLS // 128, column_sums, 0)
    total_v = jnp.sum(v_in, axis=0, keepdims=True)
    total_r = jnp.sum(in_rows[0, 1:2, :], axis=1, keepdims=True)
    stat[:, HALF:NSTAT] = jnp.where(iota((8, NSTAT - HALF), 0) == 0, total_v, total_r)

    mid = NSTAT // 2
    one, two = pl.ds(0, mid), pl.ds(mid, mid)
    stat_x[mx, :, one] = stat[:, one]
    stat_y[my, :, two] = stat[:, two]
    for d in range(1, SIDE):
        remote(stat.at[:, one], stat_x.at[mx, :, one], 44, x_peer(d))
        remote(stat.at[:, two], stat_y.at[my, :, two], 45, y_peer(d))
    all_of(stat_x.at[0:3, :, one], rsem.at[44])
    part = stat_x[0, :, one] + stat_x[1, :, one] + stat_x[2, :, one] + stat_x[3, :, one]
    stat_y[my, :, one] = part
    for d in range(1, SIDE):
        mine = stat_y.at[my, :, one]
        remote(mine, mine, 46, y_peer(d))
    all_of(stat_y.at[0:3, :, two], rsem.at[45])
    part = stat_y[0, :, two] + stat_y[1, :, two] + stat_y[2, :, two] + stat_y[3, :, two]
    stat_x[mx, :, two] = part
    for d in range(1, SIDE):
        mine = stat_x.at[mx, :, two]
        remote(mine, mine, 47, x_peer(d))

    def combine(weights, recv, exact):
        rows = unpack(recv[...])
        if exact:
            return tn(weights.astype(BF16), rows)
        high = weights.astype(BF16)
        low = (weights - high.astype(F32)).astype(BF16)
        return tn(high, rows) + tn(low, rows)

    all_of(recv_o, rsem.at[40])
    all_of(recv_o1, rsem.at[41])
    output[...] = (
        combine(gated[...], recv_o, False) + combine(gated1[...], recv_o1, False)
    ).astype(BF16)
    all_of(recv_i, rsem.at[42])
    all_of(recv_i1, rsem.at[43])
    grad_tokens[...] = (
        combine(pick[...], recv_i, True) + combine(pick1[...], recv_i1, True)
    ).astype(BF16)

    all_of(stat_y.at[0:3, :, one], rsem.at[46])
    sums[:, one] = stat_y[0, :, one] + stat_y[1, :, one] + stat_y[2, :, one] + stat_y[3, :, one]
    all_of(stat_x.at[0:3, :, two], rsem.at[47])
    sums[:, two] = stat_x[0, :, two] + stat_x[1, :, two] + stat_x[2, :, two] + stat_x[3, :, two]

    for q, src in ((0, send_x), (1, send_c)):
        all_of(src.at[0, 0 : NE - 1], ssem.at[2 * q])
        pl.when(hot)(lambda: all_of(src.at[1, 0 : n_hot - 1], ssem.at[2 * q + 1]))
        pl.when(jnp.logical_not(hot))(lambda: all_of(src.at[1, 0:n_hot], ssem.at[2 * q + 1]))

    def sent(b):
        for q in range(2):
            _s, width = part_cols(q)
            g0, _w = got_cols(q)
            c0, uw = unit_cols(q)
            cols = pl.ds(g0, width)
            for half in range(2):
                k = 4 * q + 2 * b + half
                got, last = (got_a, last_a) if half == 0 else (got_b, last_b)
                all_of(got.at[b, :, :, :, cols], ssem.at[8 + k])
                all_of(last.at[b, :, :, cols], ssem.at[16 + k])
                ucols = pl.ds(c0 + half * uw, uw)
                all_of(units.at[b, 0, 0:3, :, ucols], ssem.at[24 + k])
                all_of(units.at[b, :, 0:3, :, ucols], ssem.at[32 + k])
        all_of(send_o.at[b, 0 : NE - 1], ssem.at[40 + b])
        all_of(send_i.at[b, 0 : NE - 1], ssem.at[42 + b])

    both(sent)
    for k in range(4):
        all_of(stat_x.at[0:3, :, one], ssem.at[44 + k])


def update_kernel(
    grads, w_cat, m_cat, sums, row_v, out16, grad16, in_rows, in_cols, out_rows, out_cols,
    output, grad_tokens, new_w_in, new_w_out, new_mom_in, new_mom_out,
    new_in_rows, new_in_cols, new_out_rows, new_out_cols, moment, w16, m16,
):
    output[...] = out16[...]
    grad_tokens[...] = grad16[...]
    full = DL * SIDE * SIDE
    n_in, n_out = 2 * FF, FF

    def line(k):
        return jnp.concatenate([sums[k : k + 1, 0:HALF], sums[4 + k : 5 + k, 0:HALF]], axis=1)

    sq, sq_scaled, cross, sq_mom = line(0), line(1), line(2), line(3)
    sum_v = sums[0:1, HALF : HALF + 1]
    sum_r = sums[1:2, HALF : HALF + 1]

    def state(k):
        return jnp.concatenate(
            [in_cols[0, k, 0:1, :], in_cols[0, k, 1:2, :], out_rows[0, k : k + 1, :]], axis=1
        )

    v_in, v_out = row_v[:, 0:1], row_v[:, 1:2]
    col_v = BETA_TWO * state(0) + (1.0 - BETA_TWO) * (sq / full + EPS_ONE)
    is_in = iota((1, COLS), 1) < n_in

    def total(v):
        low = jnp.sum(v[:, 0:n_in], axis=1, keepdims=True)
        return low, jnp.sum(v[:, n_in:COLS], axis=1, keepdims=True)

    mean_in = sum_v / full
    mean_out = total(col_v)[1] / n_out
    inv = 1.0 / col_v
    norm_in, norm_out = total(sq_scaled * inv)
    clip_in = jnp.maximum(1.0, jnp.sqrt(norm_in * mean_in / (full * n_in)) / CLIP_LIMIT)
    clip_out = jnp.maximum(1.0, jnp.sqrt(norm_out * mean_out / (full * n_out)) / CLIP_LIMIT)
    scale = jnp.where(is_in, jnp.sqrt(mean_in) / clip_in, jnp.sqrt(mean_out) / clip_out)
    col_s = scale * lax.rsqrt(col_v)
    keep = BETA_ONE * BETA_ONE
    residue = keep * (col_s * col_s * sq_scaled - 2.0 * col_s * cross + sq_mom) + full * EPS_TWO
    col_r = BETA_THREE * state(1) + (1.0 - BETA_THREE) * residue / full
    mean_r_in = BETA_THREE * sum_r / full + (1.0 - BETA_THREE) * total(residue)[0] / (full * n_in)
    mean_r_out = total(col_r)[1] / n_out
    root_in, root_out = lax.rsqrt(v_in), lax.rsqrt(v_out)

    def first(c0, root, scale_row):
        acc = jnp.zeros((DL, 128), F32)
        for c in range(scale_row.shape[1] // 128):
            cols = slice(c0 + c * 128, c0 + (c + 1) * 128)
            u = grads[:, cols] * root * scale_row[:, c * 128 : (c + 1) * 128]
            old = m_cat[:, cols].astype(F32)
            new = BETA_ONE * old + (1.0 - BETA_ONE) * u
            diff = u - new
            acc = acc + (diff * diff + EPS_TWO)
            moment[:, cols] = new
            m16[:, cols] = new.astype(BF16)
        return jnp.sum(acc, axis=1, keepdims=True)

    res_in = first(0, root_in, col_s[:, 0:n_in])
    res_out = first(n_in, root_out, col_s[:, n_in:COLS])
    r_in = (
        BETA_THREE * to_column(in_rows[0, 1:2, :]) + (1.0 - BETA_THREE) * res_in / n_in
    )
    r_out = (
        BETA_THREE * to_column(out_cols[0, 1:2, :]) + (1.0 - BETA_THREE) * res_out / n_out
    )
    step_in, step_out = LEARN_RATE * lax.rsqrt(r_in), LEARN_RATE * lax.rsqrt(r_out)
    col_step = lax.rsqrt(col_r) * jnp.where(is_in, jnp.sqrt(mean_r_in), jnp.sqrt(mean_r_out))
    for c in range(COLS // 128):
        cols = slice(c * 128, (c + 1) * 128)
        rows = step_in if c < n_in // 128 else step_out
        w16[:, cols] = (
            w_cat[:, cols].astype(F32) - moment[:, cols] * rows * col_step[:, cols]
        ).astype(BF16)

    even = one_hot(iota((2 * DL, DL), 0) == 2 * iota((2 * DL, DL), 1))
    odd = one_hot(iota((2 * DL, DL), 0) == 2 * iota((2 * DL, DL), 1) + 1)
    eye = one_hot(iota((DL, DL), 0) == iota((DL, DL), 1))
    for src, inner, outer in ((w16, new_w_in, new_w_out), (m16, new_mom_in, new_mom_out)):
        flat = inner.reshape(2 * DL, FF)
        for c in range(FF // 256):
            lo = slice(c * 256, (c + 1) * 256)
            hi = slice(FF + c * 256, FF + (c + 1) * 256)
            flat[:, lo] = (nn(even, src[:, lo]) + nn(odd, src[:, hi])).astype(BF16)
            third = slice(2 * FF + c * 256, 2 * FF + (c + 1) * 256)
            outer[0, lo, :] = nt(eye, src[:, third]).astype(BF16)

    new_in_rows[0, 0:1, :] = to_row(v_in)
    new_in_rows[0, 1:2, :] = to_row(r_in)
    new_out_cols[0, 0:1, :] = to_row(v_out)
    new_out_cols[0, 1:2, :] = to_row(r_out)
    for k, v in ((0, col_v), (1, col_r)):
        new_in_cols[0, k, 0:1, :] = v[:, 0:FF]
        new_in_cols[0, k, 1:2, :] = v[:, FF : 2 * FF]
        new_out_rows[0, k : k + 1, :] = v[:, 2 * FF :]


def vmem():
    return pl.BlockSpec(memory_space=pltpu.VMEM)


def main_call(mark, *operands):
    n_hot = NE // RUN
    sds = jax.ShapeDtypeStruct
    outs = (
        sds((T, DL), BF16),
        sds((T, DL), BF16),
        sds((DL, COLS), F32),
        sds((DL, COLS), BF16),
        sds((DL, COLS), BF16),
        sds((8, NSTAT), F32),
        sds((DL, 128), F32),
    )
    block = (2, NE, 2 * CAP, 128)
    wide = COLS // 2
    flat = {4: (2 * DL, FF), 6: (2 * DL, FF)}
    scratch = [
        *(pltpu.VMEM(flat.get(i, a.shape), a.dtype) for i, a in enumerate(operands)),
        pltpu.SemaphoreType.DMA((len(operands),)),
        pltpu.VMEM(block, BF16),
        pltpu.VMEM(block, BF16),
        pltpu.VMEM(block, BF16),
        pltpu.VMEM(block, BF16),
        pltpu.VMEM((2, SIDE, SIDE, TILE, DL), BF16),
        pltpu.VMEM((2, SIDE, SIDE, TILE, DL), BF16),
        pltpu.VMEM((2, DL, ROWS), BF16),
        pltpu.VMEM((2, DL, ROWS), BF16),
        pltpu.VMEM((2, SIDE, SIDE, TILE, COLS), BF16),
        pltpu.VMEM((2, SIDE - 1, SIDE, TILE, wide), BF16),
        pltpu.VMEM((2, SIDE - 1, SIDE, TILE, wide), BF16),
        pltpu.VMEM((2, SIDE, TILE, wide), BF16),
        pltpu.VMEM((2, SIDE, TILE, wide), BF16),
        pltpu.VMEM((2, SIDE, TILE, wide), F32),
        pltpu.VMEM((2, SIDE, TILE, wide), F32),
        pltpu.VMEM((2, SIDE - 1, TILE, wide), BF16),
        pltpu.VMEM((2, SIDE - 1, TILE, wide), BF16),
        pltpu.VMEM((2, SIDE, SIDE, TILE, COLS), BF16),
        pltpu.VMEM(block, BF16),
        pltpu.VMEM(block, BF16),
        pltpu.VMEM((NE, 2 * CAP, 128), BF16),
        pltpu.VMEM((NE, 2 * CAP, 128), BF16),
        pltpu.VMEM((n_hot, 2 * CAP, 128), BF16),
        pltpu.VMEM((n_hot, 2 * CAP, 128), BF16),
        pltpu.VMEM((ROWS, T), F32),
        pltpu.VMEM((n_hot * CAP, T), F32),
        pltpu.VMEM((ROWS, T), F32),
        pltpu.VMEM((n_hot * CAP, T), F32),
        pltpu.VMEM((8, NSTAT), F32),
        pltpu.VMEM((SIDE, 8, NSTAT), F32),
        pltpu.VMEM((SIDE, 8, NSTAT), F32),
        pltpu.VMEM((2, 2, TILE, FF), F32),
        pltpu.SemaphoreType.DMA((48,)),
        pltpu.SemaphoreType.DMA((48,)),
    ]
    return pl.pallas_call(
        functools.partial(main_kernel, mark),
        out_shape=outs,
        in_specs=[pl.BlockSpec(memory_space=pltpu.HBM)] * len(operands),
        out_specs=tuple(vmem() for _ in outs),
        scratch_shapes=scratch,
        compiler_params=pltpu.CompilerParams(
            collective_id=mark,
            has_side_effects=True,
            vmem_limit_bytes=32 * 2**20,
        ),
    )(*operands)


def per_device(
    tokens, cotangent, expert_ids, gate_logits, shadow_plan, w_in, w_out, mom_in, mom_out,
    in_rows, in_cols, out_rows, out_cols,
):
    operands = (
        tokens, cotangent, expert_ids.T, gate_logits.T,
        w_in, w_out, mom_in, mom_out, in_rows, out_cols,
    )
    place = jnp.sum(shadow_plan[:RUN] * jnp.arange(RUN, dtype=jnp.int32))
    branches = [functools.partial(main_call, mark) for mark in range(RUN)]
    out16, grad16, grads, w_cat, m_cat, sums, row_v = lax.switch(place, branches, *operands)
    sds = jax.ShapeDtypeStruct
    outs = (
        sds(tokens.shape, BF16),
        sds(tokens.shape, BF16),
        sds(w_in.shape, BF16),
        sds(w_out.shape, BF16),
        sds(w_in.shape, BF16),
        sds(w_out.shape, BF16),
        sds(in_rows.shape, F32),
        sds(in_cols.shape, F32),
        sds(out_rows.shape, F32),
        sds(out_cols.shape, F32),
    )
    return pl.pallas_call(
        update_kernel,
        out_shape=outs,
        in_specs=[vmem()] * 11,
        out_specs=tuple(vmem() for _ in outs),
        scratch_shapes=[
            pltpu.VMEM((DL, COLS), F32),
            pltpu.VMEM((DL, COLS), BF16),
            pltpu.VMEM((DL, COLS), BF16),
        ],
        compiler_params=pltpu.CompilerParams(vmem_limit_bytes=32 * 2**20),
    )(grads, w_cat, m_cat, sums, row_v, out16, grad16, in_rows, in_cols, out_rows, out_cols)


def solution(mesh):
    both = P("expert", "fsdp")
    rows3 = P("expert", "fsdp", None, None)
    cols3 = P("expert", None, "fsdp")
    own = P("expert", None)
    return jax.shard_map(
        per_device,
        mesh=mesh,
        in_specs=(
            both, both, own, own, P(), rows3, cols3, rows3, cols3,
            cols3, P("expert", None, None, None), P("expert", None, None), cols3,
        ),
        out_specs=(
            both, both, rows3, cols3, rows3, cols3,
            cols3, P("expert", None, None, None), P("expert", None, None), cols3,
        ),
        check_vma=False,
    )
```

```python
import functools

import jax
import jax.numpy as jnp
from jax import lax
from jax.experimental import pallas as pl
from jax.experimental.pallas import tpu as pltpu
from jax.sharding import PartitionSpec as P

BETA_ONE = 0.9
BETA_TWO = 0.999
BETA_THREE = 0.9999
EPS_ONE = 1e-30
EPS_TWO = 1e-16
CLIP_LIMIT = 1.0
LEARN_RATE = 0.01

MESH = pl.DeviceIdType.MESH
F32 = jnp.float32
BF16 = jnp.bfloat16
NE = 32
CAP = 8
RUN = 8
SIDE = 4
T = 32
DL = 256
FF = 768
ROWS = NE * CAP
TILE = ROWS // (SIDE * SIDE)
COLS = 3 * FF
NSTAT = 1280
HALF = COLS // 2


def nn(a, b):
    return jnp.dot(a, b, preferred_element_type=F32)


def nt(a, b):
    return lax.dot_general(a, b, (((1,), (1,)), ((), ())), preferred_element_type=F32)


def tn(a, b):
    return lax.dot_general(a, b, (((0,), (0,)), ((), ())), preferred_element_type=F32)


def iota(shape, dim):
    return lax.broadcasted_iota(jnp.int32, shape, dim)


def one_hot(cond):
    return jnp.where(cond, 1.0, 0.0).astype(BF16)


def to_column(v):
    n = v.shape[1]
    return jnp.sum(jnp.where(iota((n, n), 0) == iota((n, n), 1), v, 0.0), axis=1, keepdims=True)


def to_row(v):
    n = v.shape[0]
    return jnp.sum(jnp.where(iota((n, n), 0) == iota((n, n), 1), v, 0.0), axis=0, keepdims=True)


def pack(rows):
    n = rows.shape[0] // CAP
    left = rows[:, :128].reshape(n, CAP, 128)
    right = rows[:, 128:].reshape(n, CAP, 128)
    return jnp.concatenate([left, right], axis=1).astype(BF16)


def unpack(blocks):
    wide = blocks.astype(F32)
    n = wide.shape[0]
    left = wide[:, :CAP].reshape(n * CAP, 128)
    right = wide[:, CAP:].reshape(n * CAP, 128)
    return jnp.concatenate([left, right], axis=1).astype(BF16)


def all_of(view, sem):
    pltpu.make_async_copy(view, view, sem).wait()


def main_kernel(
    mark,
    tokens_h, cotangent_h, ids_h, logits_h, w_in_h, w_out_h, mom_in_h, mom_out_h, in_rows_h, out_cols_h,
    output, grad_tokens, grads, both_h, sums, row_v,
    tokens, cotangent, ids, logits, inner, outer, in_rows, out_cols, both_cat, load_sem,
    send_x, send_c, recv_x, recv_c, x_rows, c_rows, x_t, c_t, parts, got_a, got_b, mid_a, mid_b, acc_a, acc_b,
    last_a, last_b, units, send_o, send_i, recv_o, recv_i, pick, gated,
    stat, stat_x, stat_y, pre_tile, ssem, rsem,
):
    me = lax.axis_index("expert")
    fs = lax.axis_index("fsdp")
    my, mx = fs // SIDE, lax.rem(fs, SIDE)
    stride, off = RUN, mark
    n_hot = NE // stride
    hot = lax.rem(me, stride) == off

    blocks = 1 + jnp.where(hot, 1, 0)

    def both(f):
        @pl.loop(0, blocks)
        def _(b):
            f(b)

    def x_peer(d):
        return (me, my * SIDE + lax.rem(mx + d, SIDE))

    def y_peer(d):
        return (me, lax.rem(my + d, SIDE) * SIDE + mx)

    def remote(src, dst, k, dev):
        pltpu.make_async_remote_copy(
            src_ref=src, dst_ref=dst, send_sem=ssem.at[k], recv_sem=rsem.at[k],
            device_id=dev, device_id_type=MESH,
        ).start()

    w_cat, m_cat = both_cat.at[0], both_cat.at[1]
    loads = [
        pltpu.make_async_copy(src, dst, load_sem.at[i])
        for i, (src, dst) in enumerate((
            (ids_h, ids), (logits_h, logits), (tokens_h, tokens), (cotangent_h, cotangent),
            (w_in_h.reshape(2 * DL, FF), inner.at[0]), (w_out_h.at[0], outer.at[0]),
            (mom_in_h.reshape(2 * DL, FF), inner.at[1]), (mom_out_h.at[0], outer.at[1]),
            (in_rows_h, in_rows), (out_cols_h, out_cols),
        ))
    ]
    for load in loads:
        load.start()

    barrier = pltpu.get_barrier_semaphore()

    @pl.loop(1, NE)
    def _(i):
        pl.semaphore_signal(
            barrier, inc=1, device_id=(lax.rem(me + i, NE), fs), device_id_type=MESH
        )

    for d in range(1, SIDE):
        pl.semaphore_signal(barrier, inc=1, device_id=x_peer(d), device_id_type=MESH)
        pl.semaphore_signal(barrier, inc=1, device_id=y_peer(d), device_id_type=MESH)

    for load in loads[:4]:
        load.wait()
    expert = iota((NE, T), 0)
    chosen = jnp.zeros((NE, T), F32)
    gate_of = jnp.zeros((NE, T), F32)
    sig = jax.nn.sigmoid(logits[...])
    gates = sig / jnp.sum(sig, axis=0, keepdims=True)
    picks = ids[...]
    for k in range(ids.shape[0]):
        hit = picks[k : k + 1, :] == expert
        chosen = jnp.where(hit, 1.0, chosen)
        gate_of = jnp.where(hit, gates[k : k + 1, :], gate_of)
    earlier = one_hot(iota((T, T), 0) < iota((T, T), 1))
    rank = jnp.where(chosen > 0.0, nn(chosen.astype(BF16), earlier), 1e6)
    rank_hot = rank - CAP

    def selection(rank_block, gate_block, at, sx, sc):
        n = rank_block.shape[0]
        slot = iota((n, CAP, T), 1).astype(F32)
        sel = jnp.where(rank_block[:, None, :] == slot, 1.0, 0.0)
        wsel = (sel * gate_block[:, None, :]).reshape(n * CAP, T)
        sel = sel.reshape(n * CAP, T)
        pick[at : at + n * CAP] = sel
        gated[at : at + n * CAP] = wsel
        sel16 = sel.astype(BF16)
        sx[0:n] = pack(nn(sel16, tokens[...]))
        sc[0:n] = pack(nn(sel16, cotangent[...]) * jnp.sum(wsel, axis=1, keepdims=True))

    selection(rank, gate_of, 0, send_x.at[0], send_c.at[0])
    rank1 = jnp.concatenate([rank_hot[e : e + 1] for e in range(off, NE, stride)], axis=0)
    gate1 = jnp.concatenate([gate_of[e : e + 1] for e in range(off, NE, stride)], axis=0)
    selection(rank1, gate1, ROWS, send_x.at[1], send_c.at[1])

    pl.semaphore_wait(barrier, NE - 1 + 2 * (SIDE - 1))

    def dispatch(src, dst, k):
        pltpu.make_async_copy(src.at[0, me], dst.at[0, me], rsem.at[k]).start()

        @pl.loop(1, NE)
        def _(i):
            to = lax.rem(me + i, NE)
            remote(src.at[0, to], dst.at[0, me], k, (to, fs))

        @pl.loop(0, n_hot)
        def _(i):
            r = lax.rem(i + me, n_hot)
            to = r * stride + off

            @pl.when(to == me)
            def _():
                pltpu.make_async_copy(src.at[1, r], dst.at[1, me], rsem.at[k + 1]).start()

            @pl.when(to != me)
            def _():
                remote(src.at[1, r], dst.at[1, me], k + 1, (to, fs))

    dispatch(send_x, recv_x, 0)
    dispatch(send_c, recv_c, 2)

    even = one_hot(iota((DL, 2 * DL), 1) == 2 * iota((DL, 2 * DL), 0))
    odd = one_hot(iota((DL, 2 * DL), 1) == 2 * iota((DL, 2 * DL), 0) + 1)
    eye = one_hot(iota((DL, DL), 0) == iota((DL, DL), 1))

    for load in loads[4:]:
        load.wait()

    @pl.loop(0, 2)
    def _(i):
        @pl.loop(0, FF // 128)
        def _(c):
            c0 = pl.multiple_of(c * 128, 128)
            piece = inner[i, :, pl.ds(c0, 128)]
            both_cat[i, :, pl.ds(c0, 128)] = nn(even, piece).astype(BF16)
            both_cat[i, :, pl.ds(c0 + FF, 128)] = nn(odd, piece).astype(BF16)
            both_cat[i, :, pl.ds(c0 + 2 * FF, 128)] = nt(eye, outer[i, pl.ds(c0, 128), :]).astype(BF16)

    hand_on = pltpu.make_async_copy(both_cat, both_h, load_sem.at[0])
    hand_on.start()

    def part_cols(q):
        return (0, FF) if q == 0 else (2 * FF, FF // 2)

    def got_cols(q):
        return (0, FF) if q == 0 else (FF, FF // 2)

    def project(b, q):
        src, rows_ref, t_ref = (recv_x, x_rows, x_t) if q == 0 else (recv_c, c_rows, c_t)
        all_of(src.at[b], rsem.at[2 * q + b])
        rows = unpack(src[b])
        rows_ref[b] = rows.reshape(SIDE, SIDE, TILE, DL)
        start, width = part_cols(q)

        @pl.loop(0, 2 * width // 256)
        def _(c):
            c0 = pl.multiple_of(start + c * 256, 256)
            piece = nn(rows, w_cat[:, pl.ds(c0, 256)])
            parts[b, :, :, :, pl.ds(c0, 256)] = piece.reshape(SIDE, SIDE, TILE, 256).astype(BF16)

        g0, _w = got_cols(q)
        for d in range(1, SIDE):
            to_x, to_y = lax.rem(mx + d, SIDE), lax.rem(my + d, SIDE)
            remote(
                parts.at[b, :, to_x, :, pl.ds(start, width)],
                got_a.at[b, d - 1, :, :, pl.ds(g0, width)], 8 + 4 * q + 2 * b, x_peer(d),
            )
            remote(
                parts.at[b, to_y, :, :, pl.ds(start + width, width)],
                got_b.at[b, d - 1, :, :, pl.ds(g0, width)], 9 + 4 * q + 2 * b, y_peer(d),
            )

    def halfway(b, q):
        start, width = part_cols(q)
        g0, _w = got_cols(q)
        cols = pl.ds(g0, width)
        for half in range(2):
            got, mid, acc, last = (
                (got_a, mid_a, acc_a, last_a) if half == 0 else (got_b, mid_b, acc_b, last_b)
            )
            k = 8 + 4 * q + 2 * b + half
            rows_ref = x_rows if q == 0 else c_rows
            tiles = rows_ref.at[b, :, mx] if half == 0 else rows_ref.at[b, my]
            own = nn(
                tiles[...].reshape(SIDE * TILE, DL),
                w_cat[:, start + half * width : start + (half + 1) * width],
            )
            all_of(got.at[b, :, :, :, cols], rsem.at[k])
            total = own.reshape(SIDE, TILE, width)
            for d in range(SIDE - 1):
                total = total + got[b, d, :, :, cols].astype(F32)
            acc[b, :, :, cols] = total
            mid[b, :, :, cols] = total.astype(BF16)
            for d in range(1, SIDE):
                to = lax.rem((my if half == 0 else mx) + d, SIDE)
                remote(
                    mid.at[b, to, :, cols], last.at[b, d - 1, :, cols], k + 8,
                    y_peer(d) if half == 0 else x_peer(d),
                )

    def finished(b, q, half):
        g0, width = got_cols(q)
        cols = pl.ds(g0, width)
        acc, last = (acc_a, last_a) if half == 0 else (acc_b, last_b)
        all_of(last.at[b, :, :, cols], rsem.at[16 + 4 * q + 2 * b + half])
        total = acc[b, my if half == 0 else mx, :, cols]
        for d in range(SIDE - 1):
            total = total + last[b, d, :, cols].astype(F32)
        return total

    def unit_cols(q):
        return (2 * FF, FF // 2) if q == 0 else (0, FF)

    def share(b, q):
        c0, width = unit_cols(q)
        first, second = pl.ds(c0, width), pl.ds(c0 + width, width)
        for d in range(1, SIDE):
            a, z = units.at[b, my, mx, :, first], units.at[b, my, mx, :, second]
            remote(a, a, 24 + 4 * q + 2 * b, y_peer(d))
            remote(z, z, 25 + 4 * q + 2 * b, x_peer(d))

    def spread(b, q):
        c0, width = unit_cols(q)
        first, second = pl.ds(c0, width), pl.ds(c0 + width, width)
        k = 24 + 4 * q + 2 * b
        all_of(units.at[b, 0:3, 0, :, first], rsem.at[k])
        a = units.at[b, :, mx, :, first]
        for d in range(1, SIDE):
            remote(a, a, k + 8, x_peer(d))
        all_of(units.at[b, 0, 0:3, :, second], rsem.at[k + 1])
        z = units.at[b, my, :, :, second]
        for d in range(1, SIDE):
            remote(z, z, k + 9, y_peer(d))

    def gathered(b, q):
        c0, width = unit_cols(q)
        for half in range(2):
            all_of(
                units.at[b, :, 0:3, :, pl.ds(c0 + half * width, width)],
                rsem.at[32 + 4 * q + 2 * b + half],
            )

    def forward(b):
        gate_pre, up_pre = finished(b, 0, 0), finished(b, 0, 1)
        s = jax.nn.sigmoid(gate_pre)
        pre_tile[b, 0] = gate_pre
        pre_tile[b, 1] = up_pre
        units[b, my, mx, :, 2 * FF : 3 * FF] = (gate_pre * s * up_pre).astype(BF16)
        share(b, 0)

    def backward(b):
        hidden_grad = jnp.concatenate([finished(b, 1, 0), finished(b, 1, 1)], axis=1)
        gate_pre, up_pre = pre_tile[b, 0], pre_tile[b, 1]
        s = jax.nn.sigmoid(gate_pre)
        gate_grad = hidden_grad * up_pre * s * (1.0 + gate_pre * (1.0 - s))
        units[b, my, mx, :, 0:FF] = gate_grad.astype(BF16)
        units[b, my, mx, :, FF : 2 * FF] = (hidden_grad * gate_pre * s).astype(BF16)
        share(b, 1)

    def give_back(b, src, dst, k):
        place = (1 - b) * me + b * (NE + me // stride)
        pltpu.make_async_copy(src.at[b, me], dst.at[place], rsem.at[k + b]).start()

        @pl.loop(1, NE)
        def _(i):
            to = lax.rem(me + i, NE)
            remote(src.at[b, to], dst.at[place], k + b, (to, fs))

    def rows_of(b, start, width):
        return units[b, :, :, :, start : start + width].reshape(ROWS, width)

    def down(b):
        gathered(b, 0)
        out = nt(rows_of(b, 2 * FF, FF), w_cat[:, 2 * FF : 3 * FF])
        send_o[b] = pack(out)
        give_back(b, send_o, recv_o, 40)

    def up(b):
        gathered(b, 1)
        out = nt(rows_of(b, 0, 2 * FF), w_cat[:, 0 : 2 * FF])
        send_i[b] = pack(out)
        give_back(b, send_i, recv_i, 42)

    both(lambda b: project(b, 0))
    both(lambda b: project(b, 1))
    both(lambda b: halfway(b, 0))
    both(lambda b: halfway(b, 1))
    both(forward)
    both(backward)

    def transposes(b):
        x_t[b] = x_rows[b].reshape(ROWS, DL).astype(F32).T.astype(BF16)
        c_t[b] = c_rows[b].reshape(ROWS, DL).astype(F32).T.astype(BF16)

    both(transposes)
    both(lambda b: spread(b, 0))
    both(lambda b: spread(b, 1))
    both(down)
    both(up)

    def gradients(b):
        @pl.loop(0, COLS // 256)
        def _(c):
            cols = pl.ds(pl.multiple_of(c * 256, 256), 256)
            right = units[b, :, :, :, cols].reshape(ROWS, 256)

            def put(left):
                g = nn(left, right)
                grads[:, cols] = jnp.where(b == 0, 0.0, grads[:, cols]) + g

            @pl.when(c < 2 * FF // 256)
            def _():
                put(x_t[b])

            @pl.when(c >= 2 * FF // 256)
            def _():
                put(c_t[b])

    both(gradients)

    def square_rows(c0, n):
        def step(c, total):
            g = grads[:, pl.ds(pl.multiple_of(c0 + c * 128, 128), 128)]
            return total + g * g

        total = lax.fori_loop(0, n // 128, step, jnp.zeros((DL, 128), F32))
        return jnp.sum(total, axis=1, keepdims=True) / n + EPS_ONE

    kept_in = to_column(in_rows[0, 0:1, :])
    kept_out = to_column(out_cols[0, 0:1, :])
    v_in = BETA_TWO * kept_in + (1.0 - BETA_TWO) * square_rows(0, 2 * FF)
    v_out = BETA_TWO * kept_out + (1.0 - BETA_TWO) * square_rows(2 * FF, FF)
    row_v[...] = jnp.where(iota((DL, 128), 1) == 0, v_in, v_out)
    root_in, root_out = lax.rsqrt(v_in), lax.rsqrt(v_out)

    def column_sums(c, carry):
        cols = pl.ds(pl.multiple_of(c * 128, 128), 128)
        g = grads[:, cols]
        m = m_cat[:, cols].astype(F32)
        r = jnp.where(c < 2 * FF // 128, root_in, root_out)
        gr = g * r
        four = [jnp.sum(v, axis=0, keepdims=True) for v in (g * g, gr * gr, gr * m, m * m)]
        low = c >= HALF // 128
        at = pl.ds(pl.multiple_of((c - jnp.where(low, HALF // 128, 0)) * 128, 128), 128)
        block = jnp.concatenate(four, axis=0)

        @pl.when(low)
        def _():
            stat[4:8, at] = block

        @pl.when(jnp.logical_not(low))
        def _():
            stat[0:4, at] = block

        return carry

    lax.fori_loop(0, COLS // 128, column_sums, 0)
    total_v = jnp.sum(v_in, axis=0, keepdims=True)
    total_r = jnp.sum(in_rows[0, 1:2, :], axis=1, keepdims=True)
    stat[:, HALF:NSTAT] = jnp.where(iota((8, NSTAT - HALF), 0) == 0, total_v, total_r)

    mid = NSTAT // 2
    one, two = pl.ds(0, mid), pl.ds(mid, mid)
    stat_x[mx, :, one] = stat[:, one]
    stat_y[my, :, two] = stat[:, two]
    for d in range(1, SIDE):
        remote(stat.at[:, one], stat_x.at[mx, :, one], 44, x_peer(d))
        remote(stat.at[:, two], stat_y.at[my, :, two], 45, y_peer(d))
    all_of(stat_x.at[0:3, :, one], rsem.at[44])
    part = stat_x[0, :, one] + stat_x[1, :, one] + stat_x[2, :, one] + stat_x[3, :, one]
    stat_y[my, :, one] = part
    for d in range(1, SIDE):
        mine = stat_y.at[my, :, one]
        remote(mine, mine, 46, y_peer(d))
    all_of(stat_y.at[0:3, :, two], rsem.at[45])
    part = stat_y[0, :, two] + stat_y[1, :, two] + stat_y[2, :, two] + stat_y[3, :, two]
    stat_x[mx, :, two] = part
    for d in range(1, SIDE):
        mine = stat_x.at[mx, :, two]
        remote(mine, mine, 47, x_peer(d))

    def combine(weights, recv, exact):
        rows = unpack(recv[...])
        if exact:
            return tn(weights.astype(BF16), rows)
        high = weights.astype(BF16)
        low = (weights - high.astype(F32)).astype(BF16)
        return tn(high, rows) + tn(low, rows)

    all_of(recv_o.at[0:NE], rsem.at[40])
    all_of(recv_o.at[NE : NE + n_hot], rsem.at[41])
    output[...] = combine(gated[...], recv_o, False).astype(BF16)
    all_of(recv_i.at[0:NE], rsem.at[42])
    all_of(recv_i.at[NE : NE + n_hot], rsem.at[43])
    grad_tokens[...] = combine(pick[...], recv_i, True).astype(BF16)

    all_of(stat_y.at[0:3, :, one], rsem.at[46])
    sums[:, one] = stat_y[0, :, one] + stat_y[1, :, one] + stat_y[2, :, one] + stat_y[3, :, one]
    all_of(stat_x.at[0:3, :, two], rsem.at[47])
    sums[:, two] = stat_x[0, :, two] + stat_x[1, :, two] + stat_x[2, :, two] + stat_x[3, :, two]

    hand_on.wait()
    for q, src in ((0, send_x), (1, send_c)):
        all_of(src.at[0, 0 : NE - 1], ssem.at[2 * q])
        pl.when(hot)(lambda: all_of(src.at[1, 0 : n_hot - 1], ssem.at[2 * q + 1]))
        pl.when(jnp.logical_not(hot))(lambda: all_of(src.at[1, 0:n_hot], ssem.at[2 * q + 1]))

    def sent(b):
        for q in range(2):
            _s, width = part_cols(q)
            g0, _w = got_cols(q)
            c0, uw = unit_cols(q)
            cols = pl.ds(g0, width)
            for half in range(2):
                k = 4 * q + 2 * b + half
                got, last = (got_a, last_a) if half == 0 else (got_b, last_b)
                all_of(got.at[b, :, :, :, cols], ssem.at[8 + k])
                all_of(last.at[b, :, :, cols], ssem.at[16 + k])
                ucols = pl.ds(c0 + half * uw, uw)
                all_of(units.at[b, 0, 0:3, :, ucols], ssem.at[24 + k])
                all_of(units.at[b, :, 0:3, :, ucols], ssem.at[32 + k])
        all_of(send_o.at[b, 0 : NE - 1], ssem.at[40 + b])
        all_of(send_i.at[b, 0 : NE - 1], ssem.at[42 + b])

    both(sent)
    for k in range(4):
        all_of(stat_x.at[0:3, :, one], ssem.at[44 + k])


def update_kernel(
    grads, both_h, sums, row_v, out16, grad16, in_rows, in_cols, out_rows, out_cols,
    output, grad_tokens, new_w_in, new_w_out, new_mom_in, new_mom_out,
    new_in_rows, new_in_cols, new_out_rows, new_out_cols, moment, both_cat, both_new, load_sem,
):
    loads = [
        pltpu.make_async_copy(both_h.at[i], both_cat.at[i], load_sem.at[i]) for i in range(2)
    ]
    loads[1].start()
    loads[0].start()
    output[...] = out16[...]
    grad_tokens[...] = grad16[...]
    full = DL * SIDE * SIDE
    n_in, n_out = 2 * FF, FF

    def line(k):
        return jnp.concatenate([sums[k : k + 1, 0:HALF], sums[4 + k : 5 + k, 0:HALF]], axis=1)

    sq, sq_scaled, cross, sq_mom = line(0), line(1), line(2), line(3)
    sum_v = sums[0:1, HALF : HALF + 1]
    sum_r = sums[1:2, HALF : HALF + 1]

    def state(k):
        return jnp.concatenate(
            [in_cols[0, k, 0:1, :], in_cols[0, k, 1:2, :], out_rows[0, k : k + 1, :]], axis=1
        )

    v_in, v_out = row_v[:, 0:1], row_v[:, 1:2]
    col_v = BETA_TWO * state(0) + (1.0 - BETA_TWO) * (sq / full + EPS_ONE)
    is_in = iota((1, COLS), 1) < n_in

    def total(v):
        low = jnp.sum(v[:, 0:n_in], axis=1, keepdims=True)
        return low, jnp.sum(v[:, n_in:COLS], axis=1, keepdims=True)

    mean_in = sum_v / full
    mean_out = total(col_v)[1] / n_out
    inv = 1.0 / col_v
    norm_in, norm_out = total(sq_scaled * inv)
    clip_in = jnp.maximum(1.0, jnp.sqrt(norm_in * mean_in / (full * n_in)) / CLIP_LIMIT)
    clip_out = jnp.maximum(1.0, jnp.sqrt(norm_out * mean_out / (full * n_out)) / CLIP_LIMIT)
    scale = jnp.where(is_in, jnp.sqrt(mean_in) / clip_in, jnp.sqrt(mean_out) / clip_out)
    col_s = scale * lax.rsqrt(col_v)
    keep = BETA_ONE * BETA_ONE
    residue = keep * (col_s * col_s * sq_scaled - 2.0 * col_s * cross + sq_mom) + full * EPS_TWO
    col_r = BETA_THREE * state(1) + (1.0 - BETA_THREE) * residue / full
    mean_r_in = BETA_THREE * sum_r / full + (1.0 - BETA_THREE) * total(residue)[0] / (full * n_in)
    mean_r_out = total(col_r)[1] / n_out
    root_in, root_out = lax.rsqrt(v_in), lax.rsqrt(v_out)

    loads[1].wait()

    def first(c0, n, root):
        acc = jnp.zeros((DL, 128), F32)
        for c in range(c0 // 128, (c0 + n) // 128):
            cols = slice(c * 128, (c + 1) * 128)
            u = grads[:, cols] * root * col_s[:, cols]
            new = BETA_ONE * both_cat[1, :, cols].astype(F32) + (1.0 - BETA_ONE) * u
            diff = u - new
            moment[:, cols] = new
            both_new[1, :, cols] = new.astype(BF16)
            acc = acc + (diff * diff + EPS_TWO)
        return jnp.sum(acc, axis=1, keepdims=True)

    res_in = first(0, n_in, root_in)
    res_out = first(n_in, n_out, root_out)
    r_in = (
        BETA_THREE * to_column(in_rows[0, 1:2, :]) + (1.0 - BETA_THREE) * res_in / n_in
    )
    r_out = (
        BETA_THREE * to_column(out_cols[0, 1:2, :]) + (1.0 - BETA_THREE) * res_out / n_out
    )
    step_in, step_out = LEARN_RATE * lax.rsqrt(r_in), LEARN_RATE * lax.rsqrt(r_out)
    col_step = lax.rsqrt(col_r) * jnp.where(is_in, jnp.sqrt(mean_r_in), jnp.sqrt(mean_r_out))
    loads[0].wait()

    for c in range(COLS // 128):
        cols = slice(c * 128, (c + 1) * 128)
        rows = step_in if c < n_in // 128 else step_out
        step = moment[:, cols] * rows * col_step[:, cols]
        both_new[0, :, cols] = (both_cat[0, :, cols].astype(F32) - step).astype(BF16)

    even = one_hot(iota((2 * DL, DL), 0) == 2 * iota((2 * DL, DL), 1))
    odd = one_hot(iota((2 * DL, DL), 0) == 2 * iota((2 * DL, DL), 1) + 1)
    eye = one_hot(iota((DL, DL), 0) == iota((DL, DL), 1))

    for i, (inner, outer) in ((1, (new_mom_in, new_mom_out)), (0, (new_w_in, new_w_out))):
        flat = inner.reshape(2 * DL, FF)
        for c in range(FF // 256):
            lo = slice(c * 256, (c + 1) * 256)
            hi = slice(FF + c * 256, FF + (c + 1) * 256)
            third = slice(2 * FF + c * 256, 2 * FF + (c + 1) * 256)
            flat[:, lo] = (nn(even, both_new[i, :, lo]) + nn(odd, both_new[i, :, hi])).astype(BF16)
            outer[0, lo, :] = nt(eye, both_new[i, :, third]).astype(BF16)

    new_in_rows[0, 0:1, :] = to_row(v_in)
    new_in_rows[0, 1:2, :] = to_row(r_in)
    new_out_cols[0, 0:1, :] = to_row(v_out)
    new_out_cols[0, 1:2, :] = to_row(r_out)
    for k, v in ((0, col_v), (1, col_r)):
        new_in_cols[0, k, 0:1, :] = v[:, 0:FF]
        new_in_cols[0, k, 1:2, :] = v[:, FF : 2 * FF]
        new_out_rows[0, k : k + 1, :] = v[:, 2 * FF :]


def vmem():
    return pl.BlockSpec(memory_space=pltpu.VMEM)


def hbm():
    return pl.BlockSpec(memory_space=pltpu.HBM)


def main_call(mark, *operands):
    n_hot = NE // RUN
    sds = jax.ShapeDtypeStruct
    outs = (
        sds((T, DL), BF16),
        sds((T, DL), BF16),
        sds((DL, COLS), F32),
        sds((2, DL, COLS), BF16),
        sds((8, NSTAT), F32),
        sds((DL, 128), F32),
    )
    block = (2, NE, 2 * CAP, 128)
    wide = COLS // 2
    small = operands[:4] + operands[8:]
    loaded = [pltpu.VMEM(a.shape, a.dtype) for a in small]
    loaded[4:4] = [pltpu.VMEM((2, 2 * DL, FF), BF16), pltpu.VMEM((2, FF, DL), BF16)]
    scratch = [
        *loaded,
        pltpu.VMEM((2, DL, COLS), BF16),
        pltpu.SemaphoreType.DMA((len(operands),)),
        pltpu.VMEM(block, BF16),
        pltpu.VMEM(block, BF16),
        pltpu.VMEM(block, BF16),
        pltpu.VMEM(block, BF16),
        pltpu.VMEM((2, SIDE, SIDE, TILE, DL), BF16),
        pltpu.VMEM((2, SIDE, SIDE, TILE, DL), BF16),
        pltpu.VMEM((2, DL, ROWS), BF16),
        pltpu.VMEM((2, DL, ROWS), BF16),
        pltpu.VMEM((2, SIDE, SIDE, TILE, COLS), BF16),
        pltpu.VMEM((2, SIDE - 1, SIDE, TILE, wide), BF16),
        pltpu.VMEM((2, SIDE - 1, SIDE, TILE, wide), BF16),
        pltpu.VMEM((2, SIDE, TILE, wide), BF16),
        pltpu.VMEM((2, SIDE, TILE, wide), BF16),
        pltpu.VMEM((2, SIDE, TILE, wide), F32),
        pltpu.VMEM((2, SIDE, TILE, wide), F32),
        pltpu.VMEM((2, SIDE - 1, TILE, wide), BF16),
        pltpu.VMEM((2, SIDE - 1, TILE, wide), BF16),
        pltpu.VMEM((2, SIDE, SIDE, TILE, COLS), BF16),
        pltpu.VMEM(block, BF16),
        pltpu.VMEM(block, BF16),
        pltpu.VMEM((NE + n_hot, 2 * CAP, 128), BF16),
        pltpu.VMEM((NE + n_hot, 2 * CAP, 128), BF16),
        pltpu.VMEM((ROWS + n_hot * CAP, T), F32),
        pltpu.VMEM((ROWS + n_hot * CAP, T), F32),
        pltpu.VMEM((8, NSTAT), F32),
        pltpu.VMEM((SIDE, 8, NSTAT), F32),
        pltpu.VMEM((SIDE, 8, NSTAT), F32),
        pltpu.VMEM((2, 2, TILE, FF), F32),
        pltpu.SemaphoreType.DMA((48,)),
        pltpu.SemaphoreType.DMA((48,)),
    ]
    return pl.pallas_call(
        functools.partial(main_kernel, mark),
        out_shape=outs,
        in_specs=[hbm()] * len(operands),
        out_specs=tuple(hbm() if i == 3 else vmem() for i in range(len(outs))),
        scratch_shapes=scratch,
        compiler_params=pltpu.CompilerParams(
            collective_id=mark,
            has_side_effects=True,
            vmem_limit_bytes=24 * 2**20,
        ),
    )(*operands)


def per_device(
    tokens, cotangent, expert_ids, gate_logits, shadow_plan, w_in, w_out, mom_in, mom_out,
    in_rows, in_cols, out_rows, out_cols,
):
    operands = (
        tokens, cotangent, expert_ids.T, gate_logits.T,
        w_in, w_out, mom_in, mom_out, in_rows, out_cols,
    )
    place = jnp.sum(shadow_plan[:RUN] * jnp.arange(RUN, dtype=jnp.int32))
    branches = [functools.partial(main_call, mark) for mark in range(RUN)]
    out16, grad16, grads, both_cat, sums, row_v = lax.switch(place, branches, *operands)
    sds = jax.ShapeDtypeStruct
    outs = (
        sds(tokens.shape, BF16),
        sds(tokens.shape, BF16),
        sds(w_in.shape, BF16),
        sds(w_out.shape, BF16),
        sds(w_in.shape, BF16),
        sds(w_out.shape, BF16),
        sds(in_rows.shape, F32),
        sds(in_cols.shape, F32),
        sds(out_rows.shape, F32),
        sds(out_cols.shape, F32),
    )
    return pl.pallas_call(
        update_kernel,
        out_shape=outs,
        in_specs=[hbm() if i == 1 else vmem() for i in range(10)],
        out_specs=tuple(vmem() for _ in outs),
        scratch_shapes=[
            pltpu.VMEM((DL, COLS), F32),
            pltpu.VMEM((2, DL, COLS), BF16),
            pltpu.VMEM((2, DL, COLS), BF16),
            pltpu.SemaphoreType.DMA((2,)),
        ],
        compiler_params=pltpu.CompilerParams(vmem_limit_bytes=24 * 2**20),
    )(grads, both_cat, sums, row_v, out16, grad16, in_rows, in_cols, out_rows, out_cols)


def solution(mesh):
    both = P("expert", "fsdp")
    rows3 = P("expert", "fsdp", None, None)
    cols3 = P("expert", None, "fsdp")
    own = P("expert", None)
    return jax.shard_map(
        per_device,
        mesh=mesh,
        in_specs=(
            both, both, own, own, P(), rows3, cols3, rows3, cols3,
            cols3, P("expert", None, None, None), P("expert", None, None), cols3,
        ),
        out_specs=(
            both, both, rows3, cols3, rows3, cols3,
            cols3, P("expert", None, None, None), P("expert", None, None), cols3,
        ),
        check_vma=False,
    )
```
